512 devices in a mesh: region: 16 (over y, core), tile: 32 (over x, z).
Axes of the slice: x: 4, y: 8, z: 8, core: 2. Of those that a mesh axis runs over, the one named last changes fastest.
Arguments:
- prior_pressure: float32 [64, 4, 64, 4096], P(None, None, 'region', 'tile'), may hold values from -6 to 6
- infiltration_source: float32 [64, 64, 4096], P(None, 'region', 'tile'), may hold values from -6 to 6
- soil_class: int32 [4, 64, 4096], P(None, 'region', 'tile'), may hold values from 0 to 11
- soil_k: float32 [12], replicated, may hold values from 0.02 to 0.2
- obs_index: int32 [131072], P(('region', 'tile')), may hold values from 0 to 2047
- obs_value: float32 [131072], P(('region', 'tile')), may hold values from -6 to 6
- obs_var: float32 [131072], P(('region', 'tile')), may hold values from 0.5 to 8
- obs_count: int32 [512], P(('region', 'tile')), may hold values from 1 to 256, as said below
Outputs:
- analysis: float32 [64, 4, 64, 4096], P(None, None, 'region', 'tile')
The draws below stay inside these ranges and needn't reach their ends.
Inputs may be any that keep to these rules, and one draw needn't show every extreme that they name: `obs_count`: at least one block has all 256 slots live.
All inputs are finite; a program needn't handle non-finite values.
Results may differ from the reference program's by a relative error of at most 0.00019.
Values sent between devices are 32-bit elements; how exact they have to be, the bound alone decides.
No kernel may reach another device: no remote copies, remote signals or barrier semaphores. Data moves between devices by JAX's collectives and lax.ppermute only.
A program may use at most 64 MiB of HBM per device.

```python
import math
import jax
import jax.numpy as jnp
from jax import lax

MEMBER_COUNT_N = 64
LEV = 4
ROWS_DEV = 4
COLS_DEV = 128
OBS_DEV = 256
NCLASS = 12
STEPS = 3
NR = 64
NC = 4096
NDEV = 512
NOBS = 131072
N_TILE = 32


def draw_obs_count(key, part):
    key = jax.random.fold_in(key, 7)
    values = jax.random.randint(key, (NDEV,), 1, OBS_DEV + 1, dtype=jnp.int32)
    return values.at[0].set(OBS_DEV)


def place_ends(entries, own_key, smallest, largest):
    place = [jax.random.randint(jax.random.fold_in(own_key, axis), (), 0, length) for axis, length in enumerate(entries.shape)]
    widest = entries.shape.index(max(entries.shape))
    next_to = place[:widest] + [(place[widest] + 1) % entries.shape[widest]] + place[widest + 1:]
    return entries.at[tuple(place)].set(smallest).at[tuple(next_to)].set(largest)


def steps_of(rng, extent, split, least, high):
    def one(dim, blocks):
        steps = jax.random.uniform(jax.random.fold_in(jax.random.fold_in(rng, 6), dim), (blocks,), jnp.float32, least / len(split), high / len(split))
        return jnp.repeat(jnp.exp(steps), extent[dim] // blocks).reshape((-1,) + (1,) * (len(extent) - dim - 1))

    factor_of = one(*split[0])
    for cut in split[1:]:
        factor_of = factor_of * one(*cut)
    return factor_of


def noise(rng, extent, spread, limit, shards=(), kind=jnp.bfloat16):
    values = jax.random.normal(rng, extent, jnp.float32) * spread
    if len(shards) > 0:
        values = steps_of(rng, extent, shards, -0.22, 0.18) * values
    return jnp.clip(values, min=-limit, max=limit).astype(kind)


def setup_inputs(seed: int = 0) -> dict:
    keys = jax.random.split(jax.random.key(seed), 9)
    return {
        "prior_pressure": noise(keys[0], (MEMBER_COUNT_N, LEV, NR, NC), 1.0, 6.0, ((2, 16), (3, 32)), jnp.float32),
        "infiltration_source": noise(keys[1], (MEMBER_COUNT_N, NR, NC), 1.0, 6.0, ((1, 16), (2, 32)), jnp.float32),
        "soil_class": place_ends(jax.random.randint(keys[2], (LEV, NR, NC), 0, NCLASS), jax.random.fold_in(keys[2], 1), 0, NCLASS - 1).astype(jnp.int32),
        "soil_k": jnp.clip(jnp.exp(jax.random.uniform(keys[3], (NCLASS,), jnp.float32, math.log(0.02), math.log(0.2))), 0.02, 0.2),
        "obs_index": place_ends(jax.random.randint(keys[4], (NOBS,), 0, LEV * ROWS_DEV * COLS_DEV), jax.random.fold_in(keys[4], 1), 0, (LEV * ROWS_DEV * COLS_DEV) - 1).astype(jnp.int32),
        "obs_value": noise(keys[5], (NOBS,), 1.0, 6.0, ((0, 512),), jnp.float32),
        "obs_var": jnp.clip(jnp.exp(math.log(8.0) - 2.7725887 * jax.random.uniform(keys[6], (NOBS,), jnp.float32) ** steps_of(keys[6], (NOBS,), ((0, 512),), -0.2, 0.2)), 0.5, 8.0),
        "obs_count": draw_obs_count(jax.random.fold_in(keys[8], 71), 0),
    }


step_dt = 0.25
vert_share = 0.5

def lookup(soil_class, soil_k):
    total = jnp.zeros(soil_class.shape, jnp.float32)
    for index in range(NCLASS):
        total = total + jnp.where(soil_class == index, soil_k[index], 0.0)
    return total

def cholesky_lower(matrix):
    order = matrix.shape[0]
    places = jnp.arange(order, dtype=jnp.int32)

    def column_step(column, lower):
        onehot = (places == column.astype(jnp.int32)).astype(matrix.dtype)
        row_now = jnp.dot(onehot, lower, precision=lax.Precision.HIGHEST)
        remain = jnp.dot(matrix, onehot, precision=lax.Precision.HIGHEST) - jnp.dot(lower, row_now, precision=lax.Precision.HIGHEST)
        pivot = jnp.sqrt(jnp.sum(remain * onehot))
        fresh = jnp.where(places >= column.astype(jnp.int32), remain / pivot, jnp.zeros_like(remain))
        return lower + fresh[:, None] * onehot[None, :]
    return lax.fori_loop(0, order, column_step, jnp.zeros_like(matrix))

def lower_inverse(lower):
    order = lower.shape[0]
    places = jnp.arange(order, dtype=jnp.int32)

    def row_step(row, solved):
        onehot = (places == row.astype(jnp.int32)).astype(lower.dtype)
        row_now = jnp.dot(onehot, lower, precision=lax.Precision.HIGHEST)
        pivot = jnp.sum(row_now * onehot)
        fresh = (onehot - jnp.dot(row_now, solved, precision=lax.Precision.HIGHEST)) / pivot
        return solved + onehot[:, None] * fresh[None, :]
    return lax.fori_loop(0, order, row_step, jnp.zeros_like(lower))

def propagate_pressure(state, bordered_permeability, infiltration_source):
    padded = jnp.pad(state, ((0, 0), (1, 1), (1, 1)))
    cond = bordered_permeability * (0.5 + jax.nn.sigmoid(padded))
    center = padded[:, 1:-1, 1:-1]
    kcen = cond[:, 1:-1, 1:-1]
    flux = jnp.zeros_like(center)
    for rows, cols in ((slice(2, None), slice(1, -1)), (slice(None, -2), slice(1, -1)), (slice(1, -1), slice(2, None)), (slice(1, -1), slice(None, -2))):
        flux = flux + 0.5 * (kcen + cond[:, rows, cols]) * (padded[:, rows, cols] - center)
    upward = vert_share * 0.5 * (kcen[1:] + kcen[:-1]) * (center[1:] - center[:-1])
    flux = flux + jnp.pad(upward, ((0, 1), (0, 0), (0, 0))) - jnp.pad(upward, ((1, 0), (0, 0), (0, 0)))
    flux = flux + jnp.pad(infiltration_source[None], ((0, LEV - 1), (0, 0), (0, 0)))
    return center + step_dt * flux

def reference(prior_pressure, infiltration_source, soil_class, soil_k, obs_index, obs_value, obs_var, obs_count):
    bordered_permeability = jnp.pad(lookup(soil_class, soil_k), ((0, 0), (1, 1), (1, 1)))

    def realization(pair):
        state, push = pair
        for step in range(STEPS):
            state = propagate_pressure(state, bordered_permeability, push)
        return state
    predicted_pressure = lax.map(realization, (prior_pressure, infiltration_source))
    slot = jnp.arange(NOBS, dtype=jnp.int32)
    block = slot // OBS_DEV
    depth_slab = obs_index // (ROWS_DEV * COLS_DEV)
    rest = obs_index % (ROWS_DEV * COLS_DEV)
    northing_position = block // N_TILE * ROWS_DEV + rest // COLS_DEV
    lateral_position = block % N_TILE * COLS_DEV + rest % COLS_DEV
    measured_pressure = predicted_pressure[:, depth_slab, northing_position, lateral_position]
    live = (slot % OBS_DEV < obs_count[block]).astype(jnp.float32)
    weight = live / jnp.sqrt(obs_var)
    hmean = lax.optimization_barrier(jnp.mean(measured_pressure, axis=0))
    anomal = (measured_pressure - hmean) * weight
    innov = (obs_value - hmean) * weight
    gram = jnp.dot(anomal, anomal.T, precision=lax.Precision.HIGHEST)
    bvec = jnp.dot(anomal, innov, precision=lax.Precision.HIGHEST)
    eye = jnp.eye(MEMBER_COUNT_N, dtype=jnp.float32)
    lower = cholesky_lower((MEMBER_COUNT_N - 1.0) * eye + gram)
    inverse = lower_inverse(lower)
    wmean = jnp.dot(inverse.T, jnp.dot(inverse, bvec, precision=lax.Precision.HIGHEST), precision=lax.Precision.HIGHEST)
    wroot = inverse.T * jnp.sqrt(MEMBER_COUNT_N - 1.0)
    blending_factor = wroot + wmean[:, None]
    sample_average = lax.optimization_barrier(jnp.mean(predicted_pressure, axis=0))
    deviation_matrix = (predicted_pressure - sample_average).reshape(MEMBER_COUNT_N, -1)
    propagated_vector = jnp.dot(blending_factor.T, deviation_matrix, precision=lax.Precision.HIGHEST).reshape(predicted_pressure.shape)
    return sample_average + propagated_vector
```

```python
import functools

import jax
import jax.numpy as jnp
from jax import lax
from jax.experimental import pallas as pl
from jax.experimental.pallas import tpu as pltpu
from jax.sharding import PartitionSpec as P

STEPS = 3
MEM = 64
LEV = 4
ROWS = 4
COLS = 128
GROUPS = MEM // 8
CELLS = LEV * ROWS
HALO = 3
EXT = ROWS + 2 * HALO
PAD = 72
MSG_FORCE = LEV * HALO * MEM
MSG_KC = MSG_FORCE + 2 * MEM
MSG_EDGE = MSG_KC + CELLS
MSG_ROWS = MSG_EDGE + PAD
PAYLOAD = 20
HIGHEST = lax.Precision.HIGHEST
F32 = jnp.float32


def roll(x, shift):
    shift = shift % COLS
    return x if shift == 0 else pltpu.roll(x, shift, 1)


def lanes(rows=8):
    return lax.broadcasted_iota(jnp.int32, (rows, COLS), 1)


def edge_pack(rows_of):
    lane = lanes()
    out = jnp.zeros((8, COLS), F32)
    for l in range(LEV + 1):
        for r in range(ROWS):
            block = rows_of(l, r)
            if block is None:
                continue
            start = l * 24 + r * 6
            out = jnp.where((lane >= start) & (lane < start + 6), roll(block, 3 + start), out)
    return out


def pack_kernel(h_ref, f_ref, cls_ref, k_ref, up_ref, dn_ref, edge_ref, kc_ref):
    cls = cls_ref[...]
    kc = jnp.zeros(cls.shape, F32)
    for index in range(12):
        kc = jnp.where(cls == index, k_ref[index], kc)
    kc_ref[...] = kc
    up_ref[pl.ds(MSG_KC, CELLS), :] = kc
    dn_ref[pl.ds(MSG_KC, CELLS), :] = kc
    kedge = edge_pack(
        lambda l, r: None
        if l == LEV
        else jnp.broadcast_to(kc[l * ROWS + r : l * ROWS + r + 1, :], (8, COLS))
    )
    edge_ref[pl.ds(MEM, 8), :] = kedge
    up_ref[pl.ds(MSG_EDGE + MEM, 8), :] = kedge
    dn_ref[pl.ds(MSG_EDGE + MEM, 8), :] = kedge

    for g in range(GROUPS):
        h = {}
        for l in range(LEV):
            for r in range(ROWS):
                block = h_ref[pl.ds(g * 8 * CELLS + l * ROWS + r, 8, stride=CELLS), :]
                h[l, r] = block
                if r < HALO:
                    up_ref[pl.ds((l * HALO + r) * MEM + g * 8, 8), :] = block
                if r >= ROWS - HALO:
                    dn_ref[pl.ds((l * HALO + r - 1) * MEM + g * 8, 8), :] = block
        for r in range(ROWS):
            block = f_ref[pl.ds(g * 8 * ROWS + r, 8, stride=ROWS), :]
            h[LEV, r] = block
            if r < 2:
                up_ref[pl.ds(MSG_FORCE + r * MEM + g * 8, 8), :] = block
            else:
                dn_ref[pl.ds(MSG_FORCE + (r - 2) * MEM + g * 8, 8), :] = block
        edge = edge_pack(lambda l, r: h[l, r])
        edge_ref[pl.ds(g * 8, 8), :] = edge
        up_ref[pl.ds(MSG_EDGE + g * 8, 8), :] = edge
        dn_ref[pl.ds(MSG_EDGE + g * 8, 8), :] = edge


def obs_kernel(idx_ref, val_ref, var_ref, cnt_ref, out_ref):
    slots = idx_ref.shape[1]
    idx = idx_ref[...]
    slot = lax.broadcasted_iota(jnp.int32, (1, slots), 1)
    weight = jnp.where(slot < cnt_ref[0], 1.0 / var_ref[...], 0.0)
    high = idx // COLS
    low = idx % COLS
    place = lax.broadcasted_iota(jnp.int32, (CELLS, slots), 0) == high
    lhs = jnp.concatenate(
        [jnp.where(place, weight, 0.0), jnp.where(place, weight * val_ref[...], 0.0)], axis=0
    )
    rhs = jnp.where(lax.broadcasted_iota(jnp.int32, (COLS, slots), 0) == low, 1.0, 0.0)
    out_ref[...] = lax.dot_general(
        lhs, rhs, (((1,), (1,)), ((), ())), precision=HIGHEST, preferred_element_type=F32
    )


def forecast_kernel(
    regions, tiles,
    h_ref, f_ref, kc_ref, obs_ref, above_ref, below_ref, edge_ref, el_ref, er_ref,
    uel_ref, uer_ref, del_ref, der_ref,
    dev_ref, mean_ref, pay_ref,
    z_ref, sum_ref, ks_ref, gram_ref,
):
    ri = lax.axis_index("region")
    ti = lax.axis_index("tile")
    top_ok = jnp.where(ri > 0, 1.0, 0.0)
    bot_ok = jnp.where(ri < regions - 1, 1.0, 0.0)
    left_ok = jnp.where(ti > 0, 1.0, 0.0)
    right_ok = jnp.where(ti < tiles - 1, 1.0, 0.0)
    lane = lanes()
    half = lane % 64
    srow = half // 6
    scol = half % 6
    is_left = lane < 64
    row_ok = jnp.where(srow < HALO, top_ok, jnp.where(srow >= HALO + ROWS, bot_ok, 1.0))
    side_ok = jnp.where(
        is_left, jnp.where(scol < 3, left_ok, 1.0), jnp.where(scol >= 3, right_ok, 1.0)
    )
    smask = jnp.where(half < 60, row_ok * side_ok, 0.0)
    low_k = lane % 6 < 3

    def strips(base):
        own, left, right = base(edge_ref, 0), base(el_ref, 0), base(er_ref, 0)
        uown, ul, ur = base(above_ref, MSG_EDGE), base(uel_ref, 0), base(uer_ref, 0)
        down, dl, dr = base(below_ref, MSG_EDGE), base(del_ref, 0), base(der_ref, 0)
        parts = (
            (jnp.where(low_k, ul, uown), jnp.where(low_k, uown, ur), -1),
            (jnp.where(low_k, left, own), jnp.where(low_k, own, right), 3),
            (jnp.where(low_k, dl, down), jnp.where(low_k, down, dr), 7),
        )
        out = []
        for l in range(LEV + 1):
            strip = jnp.zeros((8, COLS), F32)
            for lo, hi, first in parts:
                inside = (srow >= first) & (srow < first + ROWS)
                strip = jnp.where(inside & is_left, roll(lo, first * 6 - l * 24), strip)
                strip = jnp.where(inside & ~is_left, roll(hi, 64 + first * 6 - l * 24), strip)
            out.append(strip * smask)
        return out

    kstrip = strips(lambda ref, base: ref[pl.ds(base + MEM, 8), :])
    for l in range(LEV):
        ks_ref[pl.ds(l * 8, 8), :] = kstrip[l]
    sum_ref[...] = jnp.zeros(sum_ref.shape, F32)

    def kc_row(l, e):
        r = e - HALO
        if r < 0:
            at = MSG_KC + l * ROWS + r + ROWS
            return above_ref[at : at + 1, :] * top_ok
        if r >= ROWS:
            at = MSG_KC + l * ROWS + r - ROWS
            return below_ref[at : at + 1, :] * bot_ok
        at = l * ROWS + r
        return kc_ref[at : at + 1, :]

    kcs = {(l, e): kc_row(l, e) for l in range(LEV) for e in range(EXT)}

    def conduct(kc, h):
        return kc + (0.5 * kc) * jnp.tanh(0.5 * h)

    def group(g, carry):
        base = g * 8
        hs = strips(lambda ref, first: ref[pl.ds(first + base, 8), :])
        fs = hs[LEV]
        h = {}
        force = {}
        for l in range(LEV):
            for e in range(EXT):
                r = e - HALO
                if r < 0:
                    at = (l * HALO + r + HALO) * MEM
                    h[l, e] = above_ref[pl.ds(at + base, 8), :] * top_ok
                elif r >= ROWS:
                    at = (l * HALO + r - ROWS) * MEM
                    h[l, e] = below_ref[pl.ds(at + base, 8), :] * bot_ok
                else:
                    h[l, e] = h_ref[pl.ds(g * (8 * CELLS) + l * ROWS + r, 8, stride=CELLS), :]
        for e in range(1, EXT - 1):
            r = e - HALO
            if r < 0:
                force[e] = above_ref[pl.ds(MSG_FORCE + (r + 2) * MEM + base, 8), :]
            elif r >= ROWS:
                force[e] = below_ref[pl.ds(MSG_FORCE + (r - ROWS) * MEM + base, 8), :]
            else:
                force[e] = f_ref[pl.ds(g * (8 * ROWS) + r, 8, stride=ROWS), :]

        for step in range(STEPS):
            faces = []
            sk = [conduct(ks_ref[pl.ds(l * 8, 8), :], hs[l]) for l in range(LEV)]
            for l in range(LEV):
                faces.append((sk[l] + roll(sk[l], -1)) * (roll(hs[l], -1) - hs[l]))
            if step < STEPS - 1:
                vert = [
                    0.5 * (sk[l] + sk[l + 1]) * (hs[l + 1] - hs[l]) for l in range(LEV - 1)
                ]
                fresh = []
                for l in range(LEV):
                    down = (sk[l] + roll(sk[l], -6)) * (roll(hs[l], -6) - hs[l])
                    flux = faces[l] - roll(faces[l], 1) + down - roll(down, 6)
                    if l < LEV - 1:
                        flux = flux + vert[l]
                    if l > 0:
                        flux = flux - vert[l - 1]
                    flux = 0.125 * flux
                    if l == 0:
                        flux = flux + 0.25 * fs
                    fresh.append((hs[l] + flux) * smask)
                hs = fresh + [fs]
            k = {
                (l, e): conduct(kcs[l, e], h[l, e])
                for l in range(LEV)
                for e in range(step, EXT - step)
            }
            new = {}
            rowface = {}
            for e in range(step, EXT - step):
                above_vert = None
                for l in range(LEV):
                    if e < EXT - step - 1:
                        rowface[l, e] = (k[l, e] + k[l, e + 1]) * (h[l, e + 1] - h[l, e])
                    if e == step or e == EXT - step - 1:
                        continue
                    here, kh = h[l, e], k[l, e]
                    face = (kh + roll(kh, -1)) * (roll(here, -1) - here)
                    face = jnp.where(lane == COLS - 1, roll(faces[l], 61 - e * 6), face)
                    behind = jnp.where(lane == 0, roll(faces[l], -(e * 6 + 2)), roll(face, 1))
                    flux = (face - behind) + (rowface[l, e] - rowface[l, e - 1])
                    if l < LEV - 1:
                        vert = 0.5 * (kh + k[l + 1, e]) * (h[l + 1, e] - here)
                        flux = flux + vert
                    if l > 0:
                        flux = flux - above_vert
                    if l < LEV - 1:
                        above_vert = vert
                    flux = 0.125 * flux
                    if l == 0:
                        flux = flux + 0.25 * force[e]
                    value = here + flux
                    if e < HALO:
                        value = value * top_ok
                    elif e >= HALO + ROWS:
                        value = value * bot_ok
                    new[l, e] = value
            h = new
        for l in range(LEV):
            for r in range(ROWS):
                lr = l * ROWS + r
                value = h[l, r + HALO]
                dev_ref[pl.ds(base, 8), lr * COLS : (lr + 1) * COLS] = value
                sum_ref[lr * 8 : lr * 8 + 8, :] += value
        return carry

    lax.fori_loop(0, GROUPS, group, 0)

    for lr in range(CELLS):
        mean = jnp.sum(sum_ref[lr * 8 : lr * 8 + 8, :], axis=0, keepdims=True) * (1.0 / MEM)
        mean_ref[lr : lr + 1, :] = mean
        cols = slice(lr * COLS, (lr + 1) * COLS)
        dev = dev_ref[:, cols] - mean
        dev_ref[:, cols] = dev
        scale = obs_ref[lr : lr + 1, :]
        z_ref[0:MEM, cols] = dev * scale
        rest = obs_ref[CELLS + lr : CELLS + lr + 1, :] - scale * mean
        z_ref[MEM : MEM + 8, cols] = jnp.broadcast_to(rest, (8, COLS))
    gram_ref[:, 0:MEM] = lax.dot_general(
        z_ref[...], dev_ref[...], (((1,), (1,)), ((), ())),
        precision=HIGHEST, preferred_element_type=F32,
    )
    gram_ref[:, MEM:COLS] = jnp.zeros((PAD, COLS - MEM), F32)

    def stripe(i):
        return gram_ref[8 * i : 8 * i + 8, :]

    def joined(i):
        if i == 0:
            return stripe(0)
        other = stripe(8 - i)
        return jnp.where(lane >= 8 * i, stripe(i), roll(other, 8 * i - MEM))

    vec = stripe(8)
    sub = lax.broadcasted_iota(jnp.int32, (8, COLS), 0)
    part = jnp.where(sub % 2 == 0, vec, roll(vec, -32))
    last = jnp.where(lane >= 32, stripe(4), part)
    first = jnp.where(lane < MEM, joined(0), roll(joined(1), MEM))
    second = jnp.where(lane < MEM, joined(2), roll(joined(3), MEM))
    third = jnp.where(
        lane[0:4] < MEM, last[0:4], roll(last[4:8], MEM)
    )
    for c in range(regions):
        pay_ref[c, 0:8, :] = first
        pay_ref[c, 8:16, :] = second
        pay_ref[c, 16:20, :] = third


def analysis_kernel(copies, pay_ref, dev_ref, mean_ref, out_ref, m_ref):
    lane = lanes()
    sub = lax.broadcasted_iota(jnp.int32, (8, COLS), 0)
    first = pay_ref[0, 0:8, :]
    second = pay_ref[0, 8:16, :]
    third = pay_ref[0, 16:20, :]
    for c in range(1, copies):
        first = first + pay_ref[c, 0:8, :]
        second = second + pay_ref[c, 8:16, :]
        third = third + pay_ref[c, 16:20, :]
    halves = [
        first,
        roll(first, MEM),
        second,
        roll(second, MEM),
        jnp.concatenate([third, roll(third, MEM)], axis=0),
    ]
    for i in range(8):
        block = halves[i] if i <= 4 else roll(halves[8 - i], MEM - 8 * (8 - i))
        keep = (lane >= 8 * i) & (lane < MEM)
        block = jnp.where(keep, block, 0.0)
        block = block + jnp.where(lane == sub + 8 * i, MEM - 1.0, 0.0)
        block = block + jnp.where(lane == sub + (8 * i + MEM), 1.0, 0.0)
        m_ref[8 * i : 8 * i + 8, :] = block
    tail = halves[4]
    bvec = jnp.where(
        lane[0:1] < MEM + 32, roll(tail[0:1, :], MEM), roll(tail[1:2, :], MEM + 32)
    )

    for kb in range(8):
        block = m_ref[8 * kb : 8 * kb + 8, :]
        for j in range(8):
            at = 8 * kb + j
            inv = lax.rsqrt(block[j : j + 1, at : at + 1])
            prow = block[j : j + 1, :] * inv
            factor = block[:, at : at + 1] * inv
            block = jnp.where(
                sub > j, block - factor * prow, jnp.where(sub == j, prow, block)
            )
        m_ref[8 * kb : 8 * kb + 8, :] = block
        if kb < 7:
            later = 8 * (kb + 1)
            update = lax.dot_general(
                block[:, 0:MEM], block, (((0,), (0,)), ((), ())),
                precision=HIGHEST, preferred_element_type=F32,
            )
            m_ref[later:MEM, :] = m_ref[later:MEM, :] - update[later:MEM, :]

    inverse = m_ref[...]
    bvec = jnp.where(lane[0:1] >= MEM, bvec, 0.0)
    y = jnp.sum(inverse * bvec, axis=1, keepdims=True)
    w = jnp.sum(inverse * y, axis=0, keepdims=True)
    blend = (inverse * jnp.sqrt(jnp.full((1, COLS), MEM - 1.0, F32)) + w)[:, MEM:COLS]
    for lr in range(CELLS):
        cols = slice(lr * COLS, (lr + 1) * COLS)
        value = mean_ref[lr : lr + 1, :] + jnp.dot(
            blend, dev_ref[:, cols], precision=HIGHEST, preferred_element_type=F32
        )
        out_ref[pl.ds(lr, MEM, stride=CELLS), :] = value


def vmem():
    return pl.BlockSpec(memory_space=pltpu.VMEM)


def smem():
    return pl.BlockSpec(memory_space=pltpu.SMEM)


PARAMS = pltpu.CompilerParams(vmem_limit_bytes=32 * 1024 * 1024)


def shift(x, axis, by):
    count = lax.axis_size(axis)
    return lax.ppermute(x, axis, [(i, (i + by) % count) for i in range(count)])


def shards(prior, source, soil_class, soil_k, obs_index, obs_value, obs_var, obs_count):
    regions, tiles = lax.axis_size("region"), lax.axis_size("tile")
    prior = prior.reshape(MEM * CELLS, COLS)
    source = source.reshape(MEM * ROWS, COLS)
    soil_class = soil_class.reshape(CELLS, COLS)
    slots = obs_index.shape[0]

    def out(*shape):
        return jax.ShapeDtypeStruct(shape, F32)

    up, dn, edge, kc = pl.pallas_call(
        pack_kernel,
        out_shape=(out(MSG_ROWS, COLS), out(MSG_ROWS, COLS), out(PAD, COLS), out(CELLS, COLS)),
        in_specs=[vmem(), vmem(), vmem(), smem()],
        out_specs=(vmem(),) * 4,
        compiler_params=PARAMS,
        name="pack",
    )(prior, source, soil_class, soil_k)
    above = shift(dn, "region", 1)
    below = shift(up, "region", -1)
    el = shift(edge, "tile", 1)
    er = shift(edge, "tile", -1)
    uel, uer = shift(el, "region", 1), shift(er, "region", 1)
    bel, ber = shift(el, "region", -1), shift(er, "region", -1)
    obs = pl.pallas_call(
        obs_kernel,
        out_shape=out(2 * CELLS, COLS),
        in_specs=[vmem(), vmem(), vmem(), smem()],
        out_specs=vmem(),
        compiler_params=PARAMS,
        name="scatter_obs",
    )(
        obs_index.reshape(1, slots), obs_value.reshape(1, slots), obs_var.reshape(1, slots),
        obs_count,
    )
    dev, mean, pay = pl.pallas_call(
        functools.partial(forecast_kernel, regions, tiles),
        out_shape=(out(MEM, CELLS * COLS), out(CELLS, COLS), out(regions, PAYLOAD, COLS)),
        in_specs=[vmem()] * 13,
        out_specs=(vmem(),) * 3,
        scratch_shapes=[
            pltpu.VMEM((PAD, CELLS * COLS), F32),
            pltpu.VMEM((CELLS * 8, COLS), F32),
            pltpu.VMEM((LEV * 8, COLS), F32),
            pltpu.VMEM((PAD, COLS), F32),
        ],
        compiler_params=PARAMS,
        name="forecast",
    )(prior, source, kc, obs, above, below, edge, el, er, uel, uer, bel, ber)
    part = lax.all_to_all(pay, "region", 0, 0).sum(axis=0)
    pay = lax.all_to_all(jnp.broadcast_to(part, (tiles,) + part.shape), "tile", 0, 0)
    result = pl.pallas_call(
        functools.partial(analysis_kernel, tiles),
        out_shape=out(MEM * CELLS, COLS),
        in_specs=[vmem()] * 3,
        out_specs=vmem(),
        scratch_shapes=[pltpu.VMEM((MEM, COLS), F32)],
        compiler_params=PARAMS,
        name="analysis",
    )(pay, dev, mean)
    return result.reshape(MEM, LEV, ROWS, COLS)


def solution(mesh):
    return jax.shard_map(
        shards,
        mesh=mesh,
        in_specs=(
            P(None, None, "region", "tile"),
            P(None, "region", "tile"),
            P(None, "region", "tile"),
            P(),
            P(("region", "tile")),
            P(("region", "tile")),
            P(("region", "tile")),
            P(("region", "tile")),
        ),
        out_specs=P(None, None, "region", "tile"),
        check_vma=False,
    )
```

```python
import functools

import jax
import jax.numpy as jnp
from jax import lax
from jax.experimental import pallas as pl
from jax.experimental.pallas import tpu as pltpu
from jax.sharding import PartitionSpec as P

STEPS = 3
MEM = 64
LEV = 4
ROWS = 4
COLS = 128
GROUPS = MEM // 8
CELLS = LEV * ROWS
HALO = 3
EXT = ROWS + 2 * HALO
PAD = 72
MSG_FORCE = LEV * HALO * MEM
MSG_KC = MSG_FORCE + 2 * MEM
MSG_EDGE = MSG_KC + CELLS
MSG_ROWS = MSG_EDGE + PAD
PAYLOAD = 5 * COLS
HIGHEST = lax.Precision.HIGHEST
F32 = jnp.float32


def roll(x, shift):
    shift = shift % COLS
    return x if shift == 0 else pltpu.roll(x, shift, 1)


def lanes(rows=8):
    return lax.broadcasted_iota(jnp.int32, (rows, COLS), 1)


def edge_pack(rows_of):
    lane = lanes()
    out = jnp.zeros((8, COLS), F32)
    for l in range(LEV + 1):
        for r in range(ROWS):
            block = rows_of(l, r)
            if block is None:
                continue
            start = l * 24 + r * 6
            out = jnp.where((lane >= start) & (lane < start + 6), roll(block, 3 + start), out)
    return out


def pack_kernel(h_ref, f_ref, cls_ref, k_ref, up_ref, dn_ref, edge_ref, kc_ref):
    cls = cls_ref[...]
    kc = jnp.zeros(cls.shape, F32)
    for index in range(12):
        kc = jnp.where(cls == index, k_ref[index], kc)
    kc_ref[...] = kc
    up_ref[pl.ds(MSG_KC, CELLS), :] = kc
    dn_ref[pl.ds(MSG_KC, CELLS), :] = kc
    kedge = edge_pack(
        lambda l, r: None
        if l == LEV
        else jnp.broadcast_to(kc[l * ROWS + r : l * ROWS + r + 1, :], (8, COLS))
    )
    edge_ref[pl.ds(MEM, 8), :] = kedge
    up_ref[pl.ds(MSG_EDGE + MEM, 8), :] = kedge
    dn_ref[pl.ds(MSG_EDGE + MEM, 8), :] = kedge

    for g in range(GROUPS):
        h = {}
        for l in range(LEV):
            for r in range(ROWS):
                block = h_ref[pl.ds(g * 8 * CELLS + l * ROWS + r, 8, stride=CELLS), :]
                h[l, r] = block
                if r < HALO:
                    up_ref[pl.ds((l * HALO + r) * MEM + g * 8, 8), :] = block
                if r >= ROWS - HALO:
                    dn_ref[pl.ds((l * HALO + r - 1) * MEM + g * 8, 8), :] = block
        for r in range(ROWS):
            block = f_ref[pl.ds(g * 8 * ROWS + r, 8, stride=ROWS), :]
            h[LEV, r] = block
            if r < 2:
                up_ref[pl.ds(MSG_FORCE + r * MEM + g * 8, 8), :] = block
            else:
                dn_ref[pl.ds(MSG_FORCE + (r - 2) * MEM + g * 8, 8), :] = block
        edge = edge_pack(lambda l, r: h[l, r])
        edge_ref[pl.ds(g * 8, 8), :] = edge
        up_ref[pl.ds(MSG_EDGE + g * 8, 8), :] = edge
        dn_ref[pl.ds(MSG_EDGE + g * 8, 8), :] = edge


def obs_kernel(idx_ref, val_ref, var_ref, cnt_ref, out_ref):
    slots = idx_ref.shape[1]
    idx = idx_ref[...]
    slot = lax.broadcasted_iota(jnp.int32, (1, slots), 1)
    weight = jnp.where(slot < cnt_ref[0], 1.0 / var_ref[...], 0.0)
    high = idx // COLS
    low = idx % COLS
    place = lax.broadcasted_iota(jnp.int32, (CELLS, slots), 0) == high
    lhs = jnp.concatenate(
        [jnp.where(place, weight, 0.0), jnp.where(place, weight * val_ref[...], 0.0)], axis=0
    )
    rhs = jnp.where(lax.broadcasted_iota(jnp.int32, (COLS, slots), 0) == low, 1.0, 0.0)
    out_ref[...] = lax.dot_general(
        lhs, rhs, (((1,), (1,)), ((), ())), precision=HIGHEST, preferred_element_type=F32
    )


def forecast_kernel(
    regions, tiles,
    h_ref, f_ref, kc_ref, obs_ref, above_ref, below_ref, edge_ref, el_ref, er_ref,
    uel_ref, uer_ref, del_ref, der_ref,
    dev_ref, mean_ref, pay_ref,
    z_ref, ks_ref, kr_ref, face_ref, hold_ref, gram_ref,
):
    ri = lax.axis_index("region")
    ti = lax.axis_index("tile")
    top_ok = jnp.where(ri > 0, 1.0, 0.0)
    bot_ok = jnp.where(ri < regions - 1, 1.0, 0.0)
    left_ok = jnp.where(ti > 0, 1.0, 0.0)
    right_ok = jnp.where(ti < tiles - 1, 1.0, 0.0)
    lane = lanes()
    half = lane % 64
    srow = half // 6
    scol = half % 6
    is_left = lane < 64
    row_ok = jnp.where(srow < HALO, top_ok, jnp.where(srow >= HALO + ROWS, bot_ok, 1.0))
    side_ok = jnp.where(
        is_left, jnp.where(scol < 3, left_ok, 1.0), jnp.where(scol >= 3, right_ok, 1.0)
    )
    smask = jnp.where(half < 60, row_ok * side_ok, 0.0)
    low_k = lane % 6 < 3

    def strips(base):
        own, left, right = base(edge_ref, 0), base(el_ref, 0), base(er_ref, 0)
        uown, ul, ur = base(above_ref, MSG_EDGE), base(uel_ref, 0), base(uer_ref, 0)
        down, dl, dr = base(below_ref, MSG_EDGE), base(del_ref, 0), base(der_ref, 0)
        parts = (
            (jnp.where(low_k, ul, uown), jnp.where(low_k, uown, ur), -1),
            (jnp.where(low_k, left, own), jnp.where(low_k, own, right), 3),
            (jnp.where(low_k, dl, down), jnp.where(low_k, down, dr), 7),
        )
        out = []
        for l in range(LEV + 1):
            strip = jnp.zeros((8, COLS), F32)
            for lo, hi, first in parts:
                inside = (srow >= first) & (srow < first + ROWS)
                strip = jnp.where(inside & is_left, roll(lo, first * 6 - l * 24), strip)
                strip = jnp.where(inside & ~is_left, roll(hi, 64 + first * 6 - l * 24), strip)
            out.append(strip * smask)
        return out

    kstrip = strips(lambda ref, base: ref[pl.ds(base + MEM, 8), :])
    def kc_row(l, e):
        r = e - HALO
        if r < 0:
            at = MSG_KC + l * ROWS + r + ROWS
            return above_ref[at : at + 1, :] * top_ok
        if r >= ROWS:
            at = MSG_KC + l * ROWS + r - ROWS
            return below_ref[at : at + 1, :] * bot_ok
        at = l * ROWS + r
        return kc_ref[at : at + 1, :]

    for l in range(LEV):
        ks_ref[pl.ds(l * 8, 8), :] = 0.0625 * kstrip[l]
        for e in range(EXT):
            kr_ref[pl.ds((l * EXT + e) * 8, 8), :] = jnp.broadcast_to(
                0.0625 * kc_row(l, e), (8, COLS)
            )

    def conduct(kc, h):
        return kc * (2.0 + jnp.tanh(0.5 * h))

    joint = is_left & (scol == 1)

    def group(g, carry):
        base = g * 8

        def prior_row(l, e):
            r = e - HALO
            if r < 0:
                at = (l * HALO + r + HALO) * MEM
                return above_ref[pl.ds(at + base, 8), :] * top_ok
            if r >= ROWS:
                at = (l * HALO + r - ROWS) * MEM
                return below_ref[pl.ds(at + base, 8), :] * bot_ok
            return h_ref[pl.ds(g * (8 * CELLS) + l * ROWS + r, 8, stride=CELLS), :]

        def force_row(e):
            r = e - HALO
            if r < 0:
                return above_ref[pl.ds(MSG_FORCE + (r + 2) * MEM + base, 8), :]
            if r >= ROWS:
                return below_ref[pl.ds(MSG_FORCE + (r - ROWS) * MEM + base, 8), :]
            return f_ref[pl.ds(g * (8 * ROWS) + r, 8, stride=ROWS), :]

        hs = strips(lambda ref, first: ref[pl.ds(first + base, 8), :])
        fs = hs[LEV]
        for step in range(STEPS):
            sk = [conduct(ks_ref[pl.ds(l * 8, 8), :], hs[l]) for l in range(LEV)]
            faces = [
                (sk[l] + roll(sk[l], -1)) * (roll(hs[l], -1) - hs[l]) for l in range(LEV)
            ]
            for l in range(LEV):
                edge = jnp.where(joint, roll(faces[l], -65), faces[l])
                face_ref[pl.ds((step * LEV + l) * 8, 8), :] = edge
            if step == STEPS - 1:
                break
            fresh = []
            last = None
            for l in range(LEV):
                down = (sk[l] + roll(sk[l], -6)) * (roll(hs[l], -6) - hs[l])
                flux = (faces[l] - roll(faces[l], 1)) + (down - roll(down, 6))
                if l > 0:
                    flux = flux - last
                if l < LEV - 1:
                    last = 0.5 * (sk[l] + sk[l + 1]) * (hs[l + 1] - hs[l])
                    flux = flux + last
                if l == 0:
                    flux = flux + 0.25 * fs
                fresh.append((hs[l] + flux) * smask)
            hs = fresh

        for step in range(STEPS):
            def row(l, e):
                if step == 0:
                    return prior_row(l, e)
                return hold_ref[step - 1, pl.ds((l * EXT + e) * 8, 8), :]

            h_now = k_now = face_now = None
            for e in range(step, EXT - step):
                h_new = [row(l, e) for l in range(LEV)]
                k_new = [
                    conduct(kr_ref[pl.ds((l * EXT + e) * 8, 8), :], h_new[l])
                    for l in range(LEV)
                ]
                face_new = None
                if e > step:
                    face_new = [
                        (k_now[l] + k_new[l]) * (h_new[l] - h_now[l]) for l in range(LEV)
                    ]
                if e > step + 1:
                    at = e - 1
                    r = at - HALO
                    last = None
                    for l in range(LEV):
                        here, kh = h_now[l], k_now[l]
                        edge = roll(
                            face_ref[pl.ds((step * LEV + l) * 8, 8), :], -(at * 6 + 2)
                        )
                        face = (kh + roll(kh, -1)) * (roll(here, -1) - here)
                        face = jnp.where(lane == COLS - 1, edge, face)
                        behind = jnp.where(lane == 0, edge, roll(face, 1))
                        flux = (face - behind) + (face_new[l] - face_now[l])
                        if l > 0:
                            flux = flux - last
                        if l < LEV - 1:
                            last = 0.5 * (kh + k_now[l + 1]) * (h_now[l + 1] - here)
                            flux = flux + last
                        if l == 0:
                            flux = flux + 0.25 * force_row(at)
                        value = here + flux
                        if step == STEPS - 1:
                            lr = l * ROWS + r
                            dev_ref[pl.ds(base, 8), lr * COLS : (lr + 1) * COLS] = value
                            continue
                        if r < 0:
                            value = value * top_ok
                        elif r >= ROWS:
                            value = value * bot_ok
                        hold_ref[step, pl.ds((l * EXT + at) * 8, 8), :] = value
                h_now, k_now, face_now = h_new, k_new, face_new
        return carry

    lax.fori_loop(0, GROUPS, group, 0)

    for lr in range(CELLS):
        cols = slice(lr * COLS, (lr + 1) * COLS)
        head = dev_ref[:, cols]
        mean = jnp.sum(head, axis=0, keepdims=True) * (1.0 / MEM)
        mean_ref[lr : lr + 1, :] = mean
        dev = head - mean
        dev_ref[:, cols] = dev
        scale = obs_ref[lr : lr + 1, :]
        z_ref[0:MEM, cols] = dev * scale
        rest = obs_ref[CELLS + lr : CELLS + lr + 1, :] - scale * mean
        z_ref[MEM : MEM + 8, cols] = jnp.broadcast_to(rest, (8, COLS))
    gram_ref[:, 0:MEM] = lax.dot_general(
        z_ref[...], dev_ref[...], (((1,), (1,)), ((), ())),
        precision=HIGHEST, preferred_element_type=F32,
    )
    gram_ref[:, MEM:COLS] = jnp.zeros((PAD, COLS - MEM), F32)

    def stripe(i):
        return gram_ref[8 * i : 8 * i + 8, :]

    def joined(i):
        if i == 0:
            return stripe(0)
        other = stripe(8 - i)
        return jnp.where(lane >= 8 * i, stripe(i), roll(other, 8 * i - MEM))

    vec = stripe(8)
    sub = lax.broadcasted_iota(jnp.int32, (8, COLS), 0)
    part = jnp.where(sub % 2 == 0, vec, roll(vec, -32))
    last = jnp.where(lane >= 32, stripe(4), part)
    first = jnp.where(lane < MEM, joined(0), roll(joined(1), MEM))
    second = jnp.where(lane < MEM, joined(2), roll(joined(3), MEM))
    third = jnp.where(
        lane[0:4] < MEM, last[0:4], roll(last[4:8], MEM)
    )
    for c in range(regions):
        for i, piece in enumerate((first[0:4], first[4:8], second[0:4], second[4:8], third)):
            pay_ref[c, :, i * COLS : (i + 1) * COLS] = piece


def analysis_kernel(copies, pay_ref, dev_ref, mean_ref, out_ref, m_ref):
    lane = lanes()
    sub = lax.broadcasted_iota(jnp.int32, (8, COLS), 0)
    total = pay_ref[0]
    for c in range(1, copies):
        total = total + pay_ref[c]
    piece = [total[:, i * COLS : (i + 1) * COLS] for i in range(5)]
    first = jnp.concatenate(piece[0:2], axis=0)
    second = jnp.concatenate(piece[2:4], axis=0)
    third = piece[4]
    halves = [
        first,
        roll(first, MEM),
        second,
        roll(second, MEM),
        jnp.concatenate([third, roll(third, MEM)], axis=0),
    ]
    for i in range(8):
        block = halves[i] if i <= 4 else roll(halves[8 - i], MEM - 8 * (8 - i))
        keep = (lane >= 8 * i) & (lane < MEM)
        block = jnp.where(keep, block, 0.0)
        block = block + jnp.where(lane == sub + 8 * i, MEM - 1.0, 0.0)
        block = block + jnp.where(lane == sub + (8 * i + MEM), 1.0, 0.0)
        m_ref[8 * i : 8 * i + 8, :] = block
    tail = halves[4]
    bvec = jnp.where(
        lane[0:1] < MEM + 32, roll(tail[0:1, :], MEM), roll(tail[1:2, :], MEM + 32)
    )

    for kb in range(8):
        block = m_ref[8 * kb : 8 * kb + 8, :]
        at = 8 * kb
        full = {
            (i, j): jnp.broadcast_to(block[i : i + 1, at + j : at + j + 1], (8, COLS))
            for i in range(8)
            for j in range(i + 1)
        }
        for j in range(8):
            inv = lax.rsqrt(full[j, j])
            low = {i: full[i, j] * inv for i in range(j + 1, 8)}
            for i in range(j + 1, 8):
                for m in range(j + 1, i + 1):
                    full[i, m] = full[i, m] - low[i] * low[m]
            prow = jnp.broadcast_to(block[j : j + 1, :], (8, COLS)) * inv
            column = jnp.zeros((8, COLS), F32)
            for i in range(j + 1, 8):
                column = jnp.where(sub == i, low[i], column)
            block = jnp.where(sub == j, prow, block - column * prow)
        m_ref[8 * kb : 8 * kb + 8, :] = block
        if kb < 7:
            later = 8 * (kb + 1)
            update = lax.dot_general(
                block[:, 0:MEM], block, (((0,), (0,)), ((), ())),
                precision=HIGHEST, preferred_element_type=F32,
            )
            m_ref[later:MEM, :] = m_ref[later:MEM, :] - update[later:MEM, :]

    inverse = m_ref[...]
    bvec = jnp.where(lane[0:1] >= MEM, bvec, 0.0)
    y = jnp.sum(inverse * bvec, axis=1, keepdims=True)
    w = jnp.sum(inverse * y, axis=0, keepdims=True)
    blend = (inverse * jnp.sqrt(jnp.full((1, COLS), MEM - 1.0, F32)) + w)[:, MEM:COLS]
    for lr in range(CELLS):
        cols = slice(lr * COLS, (lr + 1) * COLS)
        value = mean_ref[lr : lr + 1, :] + jnp.dot(
            blend, dev_ref[:, cols], precision=HIGHEST, preferred_element_type=F32
        )
        out_ref[pl.ds(lr, MEM, stride=CELLS), :] = value


def vmem():
    return pl.BlockSpec(memory_space=pltpu.VMEM)


def smem():
    return pl.BlockSpec(memory_space=pltpu.SMEM)


PARAMS = pltpu.CompilerParams(vmem_limit_bytes=32 * 1024 * 1024)


def shift(x, axis, by):
    count = lax.axis_size(axis)
    return lax.ppermute(x, axis, [(i, (i + by) % count) for i in range(count)])


def shards(prior, source, soil_class, soil_k, obs_index, obs_value, obs_var, obs_count):
    regions, tiles = lax.axis_size("region"), lax.axis_size("tile")
    prior = prior.reshape(MEM * CELLS, COLS)
    source = source.reshape(MEM * ROWS, COLS)
    soil_class = soil_class.reshape(CELLS, COLS)
    slots = obs_index.shape[0]

    def out(*shape):
        return jax.ShapeDtypeStruct(shape, F32)

    up, dn, edge, kc = pl.pallas_call(
        pack_kernel,
        out_shape=(out(MSG_ROWS, COLS), out(MSG_ROWS, COLS), out(PAD, COLS), out(CELLS, COLS)),
        in_specs=[vmem(), vmem(), vmem(), smem()],
        out_specs=(vmem(),) * 4,
        compiler_params=PARAMS,
        name="pack",
    )(prior, source, soil_class, soil_k)
    above = shift(dn, "region", 1)
    below = shift(up, "region", -1)
    el = shift(edge, "tile", 1)
    er = shift(edge, "tile", -1)
    uel, uer = shift(el, "region", 1), shift(er, "region", 1)
    bel, ber = shift(el, "region", -1), shift(er, "region", -1)
    obs = pl.pallas_call(
        obs_kernel,
        out_shape=out(2 * CELLS, COLS),
        in_specs=[vmem(), vmem(), vmem(), smem()],
        out_specs=vmem(),
        compiler_params=PARAMS,
        name="scatter_obs",
    )(
        obs_index.reshape(1, slots), obs_value.reshape(1, slots), obs_var.reshape(1, slots),
        obs_count,
    )
    dev, mean, pay = pl.pallas_call(
        functools.partial(forecast_kernel, regions, tiles),
        out_shape=(out(MEM, CELLS * COLS), out(CELLS, COLS), out(regions, 4, PAYLOAD)),
        in_specs=[vmem()] * 13,
        out_specs=(vmem(),) * 3,
        scratch_shapes=[
            pltpu.VMEM((PAD, CELLS * COLS), F32),
            pltpu.VMEM((LEV * 8, COLS), F32),
            pltpu.VMEM((LEV * EXT * 8, COLS), F32),
            pltpu.VMEM((STEPS * LEV * 8, COLS), F32),
            pltpu.VMEM((STEPS - 1, LEV * EXT * 8, COLS), F32),
            pltpu.VMEM((PAD, COLS), F32),
        ],
        compiler_params=PARAMS,
        name="forecast",
    )(prior, source, kc, obs, above, below, edge, el, er, uel, uer, bel, ber)
    part = lax.all_to_all(pay, "region", 0, 0).sum(axis=0)
    pay = lax.all_to_all(jnp.broadcast_to(part, (tiles,) + part.shape), "tile", 0, 0)
    result = pl.pallas_call(
        functools.partial(analysis_kernel, tiles),
        out_shape=out(MEM * CELLS, COLS),
        in_specs=[vmem()] * 3,
        out_specs=vmem(),
        scratch_shapes=[pltpu.VMEM((MEM, COLS), F32)],
        compiler_params=PARAMS,
        name="analysis",
    )(pay, dev, mean)
    return result.reshape(MEM, LEV, ROWS, COLS)


def solution(mesh):
    return jax.shard_map(
        shards,
        mesh=mesh,
        in_specs=(
            P(None, None, "region", "tile"),
            P(None, "region", "tile"),
            P(None, "region", "tile"),
            P(),
            P(("region", "tile")),
            P(("region", "tile")),
            P(("region", "tile")),
            P(("region", "tile")),
        ),
        out_specs=P(None, None, "region", "tile"),
        check_vma=False,
    )
```

```python
import functools

import jax
import jax.numpy as jnp
from jax import lax
from jax.experimental import pallas as pl
from jax.experimental.pallas import tpu as pltpu
from jax.sharding import PartitionSpec as P

STEPS = 3
MEM = 64
LEV = 4
ROWS = 4
COLS = 128
GROUPS = MEM // 8
CELLS = LEV * ROWS
HALO = 3
EXT = ROWS + 2 * HALO
PAD = 72
MSG_FORCE = LEV * HALO * MEM
MSG_KC = MSG_FORCE + 2 * MEM
MSG_EDGE = MSG_KC + CELLS
MSG_ROWS = MSG_EDGE + PAD
PAYLOAD = 5 * COLS
HIGHEST = lax.Precision.HIGHEST
F32 = jnp.float32


def roll(x, shift):
    shift = shift % COLS
    return x if shift == 0 else pltpu.roll(x, shift, 1)


def lanes(rows=8):
    return lax.broadcasted_iota(jnp.int32, (rows, COLS), 1)


def edge_pack(rows_of):
    lane = lanes()
    out = jnp.zeros((8, COLS), F32)
    for l in range(LEV + 1):
        for r in range(ROWS):
            block = rows_of(l, r)
            if block is None:
                continue
            start = l * 24 + r * 6
            out = jnp.where((lane >= start) & (lane < start + 6), roll(block, 3 + start), out)
    return out


def scatter_obs(idx_ref, val_ref, var_ref, count):
    slots = idx_ref.shape[1]
    idx = idx_ref[...]
    slot = lax.broadcasted_iota(jnp.int32, (1, slots), 1)
    weight = jnp.where(slot < count, 1.0 / var_ref[...], 0.0)
    place = lax.broadcasted_iota(jnp.int32, (CELLS, slots), 0) == idx // COLS
    lhs = jnp.concatenate(
        [jnp.where(place, weight, 0.0), jnp.where(place, weight * val_ref[...], 0.0)], axis=0
    )
    rhs = jnp.where(
        lax.broadcasted_iota(jnp.int32, (COLS, slots), 0) == idx % COLS, 1.0, 0.0
    )
    return lax.dot_general(
        lhs, rhs, (((1,), (1,)), ((), ())), precision=HIGHEST, preferred_element_type=F32
    )


def pack_kernel(
    h_ref, f_ref, cls_ref, idx_ref, val_ref, var_ref, k_ref, cnt_ref,
    up_ref, dn_ref, own_ref, edge_ref,
):
    cls = cls_ref[...]
    kc = jnp.zeros(cls.shape, F32)
    for index in range(12):
        kc = jnp.where(cls == index, k_ref[index], kc)
    own_ref[pl.ds(PAD, CELLS), :] = kc
    up_ref[pl.ds(MSG_KC, CELLS), :] = kc
    dn_ref[pl.ds(MSG_KC, CELLS), :] = kc
    kedge = edge_pack(
        lambda l, r: None
        if l == LEV
        else jnp.broadcast_to(kc[l * ROWS + r : l * ROWS + r + 1, :], (8, COLS))
    )
    edge_ref[pl.ds(MEM, 8), :] = kedge
    own_ref[pl.ds(MEM, 8), :] = kedge
    up_ref[pl.ds(MSG_EDGE + MEM, 8), :] = kedge
    dn_ref[pl.ds(MSG_EDGE + MEM, 8), :] = kedge

    own_ref[pl.ds(PAD + CELLS, 2 * CELLS), :] = scatter_obs(
        idx_ref, val_ref, var_ref, cnt_ref[0]
    )
    for g in range(GROUPS):
        h = {}
        for l in range(LEV):
            for r in range(ROWS):
                block = h_ref[pl.ds(g * 8 * CELLS + l * ROWS + r, 8, stride=CELLS), :]
                h[l, r] = block
                if r < HALO:
                    up_ref[pl.ds((l * HALO + r) * MEM + g * 8, 8), :] = block
                if r >= ROWS - HALO:
                    dn_ref[pl.ds((l * HALO + r - 1) * MEM + g * 8, 8), :] = block
        for r in range(ROWS):
            block = f_ref[pl.ds(g * 8 * ROWS + r, 8, stride=ROWS), :]
            h[LEV, r] = block
            if r < 2:
                up_ref[pl.ds(MSG_FORCE + r * MEM + g * 8, 8), :] = block
            else:
                dn_ref[pl.ds(MSG_FORCE + (r - 2) * MEM + g * 8, 8), :] = block
        edge = edge_pack(lambda l, r: h[l, r])
        edge_ref[pl.ds(g * 8, 8), :] = edge
        own_ref[pl.ds(g * 8, 8), :] = edge
        up_ref[pl.ds(MSG_EDGE + g * 8, 8), :] = edge
        dn_ref[pl.ds(MSG_EDGE + g * 8, 8), :] = edge


def forecast_kernel(
    regions, tiles,
    h_ref, f_ref, own_ref, above_ref, below_ref, el_ref, er_ref,
    uel_ref, uer_ref, del_ref, der_ref,
    dev_ref, mean_ref, pay_ref,
    z_ref, ks_ref, kr_ref, face_ref, hold_ref, gram_ref,
):
    ri = lax.axis_index("region")
    ti = lax.axis_index("tile")
    top_ok = jnp.where(ri > 0, 1.0, 0.0)
    bot_ok = jnp.where(ri < regions - 1, 1.0, 0.0)
    left_ok = jnp.where(ti > 0, 1.0, 0.0)
    right_ok = jnp.where(ti < tiles - 1, 1.0, 0.0)
    lane = lanes()
    half = lane % 64
    srow = half // 6
    scol = half % 6
    is_left = lane < 64
    row_ok = jnp.where(srow < HALO, top_ok, jnp.where(srow >= HALO + ROWS, bot_ok, 1.0))
    side_ok = jnp.where(
        is_left, jnp.where(scol < 3, left_ok, 1.0), jnp.where(scol >= 3, right_ok, 1.0)
    )
    smask = jnp.where(half < 60, row_ok * side_ok, 0.0)
    low_k = lane % 6 < 3

    def strips(base):
        own, left, right = base(own_ref, 0), base(el_ref, 0), base(er_ref, 0)
        uown, ul, ur = base(above_ref, MSG_EDGE), base(uel_ref, 0), base(uer_ref, 0)
        down, dl, dr = base(below_ref, MSG_EDGE), base(del_ref, 0), base(der_ref, 0)
        parts = (
            (jnp.where(low_k, ul, uown), jnp.where(low_k, uown, ur), -1),
            (jnp.where(low_k, left, own), jnp.where(low_k, own, right), 3),
            (jnp.where(low_k, dl, down), jnp.where(low_k, down, dr), 7),
        )
        out = []
        for l in range(LEV + 1):
            strip = jnp.zeros((8, COLS), F32)
            for lo, hi, first in parts:
                inside = (srow >= first) & (srow < first + ROWS)
                strip = jnp.where(inside & is_left, roll(lo, first * 6 - l * 24), strip)
                strip = jnp.where(inside & ~is_left, roll(hi, 64 + first * 6 - l * 24), strip)
            out.append(strip * smask)
        return out

    kstrip = strips(lambda ref, base: ref[pl.ds(base + MEM, 8), :])
    def kc_row(l, e):
        r = e - HALO
        if r < 0:
            at = MSG_KC + l * ROWS + r + ROWS
            return above_ref[at : at + 1, :] * top_ok
        if r >= ROWS:
            at = MSG_KC + l * ROWS + r - ROWS
            return below_ref[at : at + 1, :] * bot_ok
        at = PAD + l * ROWS + r
        return own_ref[at : at + 1, :]

    for l in range(LEV):
        ks_ref[pl.ds(l * 8, 8), :] = 0.0625 * kstrip[l]
        for e in range(EXT):
            kr_ref[pl.ds((l * EXT + e) * 8, 8), :] = jnp.broadcast_to(
                0.0625 * kc_row(l, e), (8, COLS)
            )

    def conduct(kc, h):
        return kc * (2.0 + jnp.tanh(0.5 * h))

    joint = is_left & (scol == 1)

    def group(g, carry):
        base = g * 8

        def prior_row(l, e):
            r = e - HALO
            if r < 0:
                at = (l * HALO + r + HALO) * MEM
                return above_ref[pl.ds(at + base, 8), :] * top_ok
            if r >= ROWS:
                at = (l * HALO + r - ROWS) * MEM
                return below_ref[pl.ds(at + base, 8), :] * bot_ok
            return h_ref[pl.ds(g * (8 * CELLS) + l * ROWS + r, 8, stride=CELLS), :]

        def force_row(e):
            r = e - HALO
            if r < 0:
                return above_ref[pl.ds(MSG_FORCE + (r + 2) * MEM + base, 8), :]
            if r >= ROWS:
                return below_ref[pl.ds(MSG_FORCE + (r - ROWS) * MEM + base, 8), :]
            return f_ref[pl.ds(g * (8 * ROWS) + r, 8, stride=ROWS), :]

        hs = strips(lambda ref, first: ref[pl.ds(first + base, 8), :])
        fs = hs[LEV]
        for step in range(STEPS):
            sk = [conduct(ks_ref[pl.ds(l * 8, 8), :], hs[l]) for l in range(LEV)]
            faces = [
                (sk[l] + roll(sk[l], -1)) * (roll(hs[l], -1) - hs[l]) for l in range(LEV)
            ]
            for l in range(LEV):
                edge = jnp.where(joint, roll(faces[l], -65), faces[l])
                face_ref[pl.ds((step * LEV + l) * 8, 8), :] = edge
            if step == STEPS - 1:
                break
            fresh = []
            last = None
            for l in range(LEV):
                down = (sk[l] + roll(sk[l], -6)) * (roll(hs[l], -6) - hs[l])
                flux = (faces[l] - roll(faces[l], 1)) + (down - roll(down, 6))
                if l > 0:
                    flux = flux - last
                if l < LEV - 1:
                    last = 0.5 * (sk[l] + sk[l + 1]) * (hs[l + 1] - hs[l])
                    flux = flux + last
                if l == 0:
                    flux = flux + 0.25 * fs
                fresh.append((hs[l] + flux) * smask)
            hs = fresh

        for step in range(STEPS):
            def row(l, e):
                if step == 0:
                    return prior_row(l, e)
                return hold_ref[step - 1, pl.ds((l * EXT + e) * 8, 8), :]

            h_now = k_now = face_now = None
            for e in range(step, EXT - step):
                h_new = [row(l, e) for l in range(LEV)]
                k_new = [
                    conduct(kr_ref[pl.ds((l * EXT + e) * 8, 8), :], h_new[l])
                    for l in range(LEV)
                ]
                face_new = None
                if e > step:
                    face_new = [
                        (k_now[l] + k_new[l]) * (h_new[l] - h_now[l]) for l in range(LEV)
                    ]
                if e > step + 1:
                    at = e - 1
                    r = at - HALO
                    last = None
                    for l in range(LEV):
                        here, kh = h_now[l], k_now[l]
                        edge = roll(
                            face_ref[pl.ds((step * LEV + l) * 8, 8), :], -(at * 6 + 2)
                        )
                        face = (kh + roll(kh, -1)) * (roll(here, -1) - here)
                        face = jnp.where(lane == COLS - 1, edge, face)
                        behind = jnp.where(lane == 0, edge, roll(face, 1))
                        flux = (face - behind) + (face_new[l] - face_now[l])
                        if l > 0:
                            flux = flux - last
                        if l < LEV - 1:
                            last = 0.5 * (kh + k_now[l + 1]) * (h_now[l + 1] - here)
                            flux = flux + last
                        if l == 0:
                            flux = flux + 0.25 * force_row(at)
                        value = here + flux
                        if step == STEPS - 1:
                            lr = l * ROWS + r
                            dev_ref[pl.ds(base, 8), lr * COLS : (lr + 1) * COLS] = value
                            continue
                        if r < 0:
                            value = value * top_ok
                        elif r >= ROWS:
                            value = value * bot_ok
                        hold_ref[step, pl.ds((l * EXT + at) * 8, 8), :] = value
                h_now, k_now, face_now = h_new, k_new, face_new
        return carry

    lax.fori_loop(0, GROUPS, group, 0)

    for lr in range(CELLS):
        cols = slice(lr * COLS, (lr + 1) * COLS)
        head = dev_ref[:, cols]
        mean = jnp.sum(head, axis=0, keepdims=True) * (1.0 / MEM)
        mean_ref[lr : lr + 1, :] = mean
        dev = head - mean
        dev_ref[:, cols] = dev
        scale = own_ref[PAD + CELLS + lr : PAD + CELLS + lr + 1, :]
        z_ref[0:MEM, cols] = dev * scale
        rest = own_ref[PAD + 2 * CELLS + lr : PAD + 2 * CELLS + lr + 1, :] - scale * mean
        z_ref[MEM : MEM + 8, cols] = jnp.broadcast_to(rest, (8, COLS))
    gram_ref[:, 0:MEM] = lax.dot_general(
        z_ref[...], dev_ref[...], (((1,), (1,)), ((), ())),
        precision=HIGHEST, preferred_element_type=F32,
    )
    gram_ref[:, MEM:COLS] = jnp.zeros((PAD, COLS - MEM), F32)

    def stripe(i):
        return gram_ref[8 * i : 8 * i + 8, :]

    def joined(i):
        if i == 0:
            return stripe(0)
        other = stripe(8 - i)
        return jnp.where(lane >= 8 * i, stripe(i), roll(other, 8 * i - MEM))

    vec = stripe(8)
    sub = lax.broadcasted_iota(jnp.int32, (8, COLS), 0)
    part = jnp.where(sub % 2 == 0, vec, roll(vec, -32))
    last = jnp.where(lane >= 32, stripe(4), part)
    first = jnp.where(lane < MEM, joined(0), roll(joined(1), MEM))
    second = jnp.where(lane < MEM, joined(2), roll(joined(3), MEM))
    third = jnp.where(
        lane[0:4] < MEM, last[0:4], roll(last[4:8], MEM)
    )
    for c in range(regions):
        for i, piece in enumerate((first[0:4], first[4:8], second[0:4], second[4:8], third)):
            pay_ref[c, :, i * COLS : (i + 1) * COLS] = piece


def analysis_kernel(copies, pay_ref, dev_ref, mean_ref, out_ref, m_ref):
    lane = lanes()
    sub = lax.broadcasted_iota(jnp.int32, (8, COLS), 0)
    total = pay_ref[0]
    for c in range(1, copies):
        total = total + pay_ref[c]
    piece = [total[:, i * COLS : (i + 1) * COLS] for i in range(5)]
    first = jnp.concatenate(piece[0:2], axis=0)
    second = jnp.concatenate(piece[2:4], axis=0)
    third = piece[4]
    halves = [
        first,
        roll(first, MEM),
        second,
        roll(second, MEM),
        jnp.concatenate([third, roll(third, MEM)], axis=0),
    ]
    for i in range(8):
        block = halves[i] if i <= 4 else roll(halves[8 - i], MEM - 8 * (8 - i))
        keep = (lane >= 8 * i) & (lane < MEM)
        block = jnp.where(keep, block, 0.0)
        block = block + jnp.where(lane == sub + 8 * i, MEM - 1.0, 0.0)
        block = block + jnp.where(lane == sub + (8 * i + MEM), 1.0, 0.0)
        m_ref[8 * i : 8 * i + 8, :] = block
    tail = halves[4]
    bvec = jnp.where(
        lane[0:1] < MEM + 32, roll(tail[0:1, :], MEM), roll(tail[1:2, :], MEM + 32)
    )

    for kb in range(8):
        block = m_ref[8 * kb : 8 * kb + 8, :]
        at = 8 * kb
        full = {
            (i, j): jnp.broadcast_to(block[i : i + 1, at + j : at + j + 1], (8, COLS))
            for i in range(8)
            for j in range(i + 1)
        }
        for j in range(8):
            inv = lax.rsqrt(full[j, j])
            low = {i: full[i, j] * inv for i in range(j + 1, 8)}
            for i in range(j + 1, 8):
                for m in range(j + 1, i + 1):
                    full[i, m] = full[i, m] - low[i] * low[m]
            prow = jnp.broadcast_to(block[j : j + 1, :], (8, COLS)) * inv
            column = jnp.zeros((8, COLS), F32)
            for i in range(j + 1, 8):
                column = jnp.where(sub == i, low[i], column)
            block = jnp.where(sub == j, prow, block - column * prow)
        m_ref[8 * kb : 8 * kb + 8, :] = block
        if kb < 7:
            later = 8 * (kb + 1)
            update = lax.dot_general(
                block[:, 0:MEM], block, (((0,), (0,)), ((), ())),
                precision=HIGHEST, preferred_element_type=F32,
            )
            m_ref[later:MEM, :] = m_ref[later:MEM, :] - update[later:MEM, :]

    inverse = m_ref[...]
    bvec = jnp.where(lane[0:1] >= MEM, bvec, 0.0)
    y = jnp.sum(inverse * bvec, axis=1, keepdims=True)
    w = jnp.sum(inverse * y, axis=0, keepdims=True)
    blend = (inverse * jnp.sqrt(jnp.full((1, COLS), MEM - 1.0, F32)) + w)[:, MEM:COLS]
    for lr in range(CELLS):
        cols = slice(lr * COLS, (lr + 1) * COLS)
        value = mean_ref[lr : lr + 1, :] + jnp.dot(
            blend, dev_ref[:, cols], precision=HIGHEST, preferred_element_type=F32
        )
        out_ref[pl.ds(lr, MEM, stride=CELLS), :] = value


def vmem():
    return pl.BlockSpec(memory_space=pltpu.VMEM)


def smem():
    return pl.BlockSpec(memory_space=pltpu.SMEM)


PARAMS = pltpu.CompilerParams(vmem_limit_bytes=32 * 1024 * 1024)


def shift(x, axis, by, wrap=True):
    count = lax.axis_size(axis)
    pairs = [(i, (i + by) % count) for i in range(count) if wrap or 0 <= i + by < count]
    return lax.ppermute(x, axis, pairs)


def shards(prior, source, soil_class, soil_k, obs_index, obs_value, obs_var, obs_count):
    regions, tiles = lax.axis_size("region"), lax.axis_size("tile")
    prior = prior.reshape(MEM * CELLS, COLS)
    source = source.reshape(MEM * ROWS, COLS)
    soil_class = soil_class.reshape(CELLS, COLS)
    slots = obs_index.shape[0]

    def out(*shape):
        return jax.ShapeDtypeStruct(shape, F32)

    up, dn, own, edge = pl.pallas_call(
        pack_kernel,
        out_shape=(
            out(MSG_ROWS, COLS), out(MSG_ROWS, COLS), out(PAD + 3 * CELLS, COLS), out(PAD, COLS)
        ),
        in_specs=[vmem()] * 6 + [smem()] * 2,
        out_specs=(vmem(),) * 4,
        compiler_params=PARAMS,
        name="pack",
    )(
        prior, source, soil_class,
        obs_index.reshape(1, slots), obs_value.reshape(1, slots), obs_var.reshape(1, slots),
        soil_k, obs_count,
    )
    above = shift(dn, "region", 1)
    below = shift(up, "region", -1)
    el = shift(edge, "tile", 1, False)
    er = shift(edge, "tile", -1, False)
    uel, uer = shift(el, "region", 1), shift(er, "region", 1)
    bel, ber = shift(el, "region", -1), shift(er, "region", -1)
    dev, mean, pay = pl.pallas_call(
        functools.partial(forecast_kernel, regions, tiles),
        out_shape=(out(MEM, CELLS * COLS), out(CELLS, COLS), out(regions, 4, PAYLOAD)),
        in_specs=[vmem()] * 11,
        out_specs=(vmem(),) * 3,
        scratch_shapes=[
            pltpu.VMEM((PAD, CELLS * COLS), F32),
            pltpu.VMEM((LEV * 8, COLS), F32),
            pltpu.VMEM((LEV * EXT * 8, COLS), F32),
            pltpu.VMEM((STEPS * LEV * 8, COLS), F32),
            pltpu.VMEM((STEPS - 1, LEV * EXT * 8, COLS), F32),
            pltpu.VMEM((PAD, COLS), F32),
        ],
        compiler_params=PARAMS,
        name="forecast",
    )(prior, source, own, above, below, el, er, uel, uer, bel, ber)
    part = lax.all_to_all(pay, "region", 0, 0).sum(axis=0)
    pay = lax.all_to_all(jnp.broadcast_to(part, (tiles,) + part.shape), "tile", 0, 0)
    result = pl.pallas_call(
        functools.partial(analysis_kernel, tiles),
        out_shape=out(MEM * CELLS, COLS),
        in_specs=[vmem()] * 3,
        out_specs=vmem(),
        scratch_shapes=[pltpu.VMEM((MEM, COLS), F32)],
        compiler_params=PARAMS,
        name="analysis",
    )(pay, dev, mean)
    return result.reshape(MEM, LEV, ROWS, COLS)


def solution(mesh):
    return jax.shard_map(
        shards,
        mesh=mesh,
        in_specs=(
            P(None, None, "region", "tile"),
            P(None, "region", "tile"),
            P(None, "region", "tile"),
            P(),
            P(("region", "tile")),
            P(("region", "tile")),
            P(("region", "tile")),
            P(("region", "tile")),
        ),
        out_specs=P(None, None, "region", "tile"),
        check_vma=False,
    )
```

```python
import functools

import jax
import jax.numpy as jnp
from jax import lax
from jax.experimental import pallas as pl
from jax.experimental.pallas import tpu as pltpu
from jax.sharding import PartitionSpec as P

STEPS = 3
MEM = 64
LEV = 4
ROWS = 4
COLS = 128
GROUPS = MEM // 8
CELLS = LEV * ROWS
HALO = 3
EXT = ROWS + 2 * HALO
PAD = 72
MSG_FORCE = LEV * HALO * MEM
MSG_KC = MSG_FORCE + 2 * MEM
MSG_EDGE = MSG_KC + CELLS
MSG_ROWS = MSG_EDGE + PAD
PAYLOAD = 9 * COLS
HIGHEST = lax.Precision.HIGHEST
F32 = jnp.float32


def roll(x, shift):
    shift = shift % COLS
    return x if shift == 0 else pltpu.roll(x, shift, 1)


def lanes(rows=8):
    return lax.broadcasted_iota(jnp.int32, (rows, COLS), 1)


def edge_pack(rows_of):
    lane = lanes()
    out = jnp.zeros((8, COLS), F32)
    for l in range(LEV + 1):
        for r in range(ROWS):
            block = rows_of(l, r)
            if block is None:
                continue
            start = l * 24 + r * 6
            out = jnp.where((lane >= start) & (lane < start + 6), roll(block, 3 + start), out)
    return out


def scatter_obs(idx_ref, val_ref, var_ref, count):
    slots = idx_ref.shape[1]
    idx = idx_ref[...]
    slot = lax.broadcasted_iota(jnp.int32, (1, slots), 1)
    weight = jnp.where(slot < count, 1.0 / var_ref[...], 0.0)
    place = lax.broadcasted_iota(jnp.int32, (CELLS, slots), 0) == idx // COLS
    lhs = jnp.concatenate(
        [jnp.where(place, weight, 0.0), jnp.where(place, weight * val_ref[...], 0.0)], axis=0
    )
    rhs = jnp.where(
        lax.broadcasted_iota(jnp.int32, (COLS, slots), 0) == idx % COLS, 1.0, 0.0
    )
    return lax.dot_general(
        lhs, rhs, (((1,), (1,)), ((), ())), precision=HIGHEST, preferred_element_type=F32
    )


def pack_kernel(
    h_ref, f_ref, cls_ref, idx_ref, val_ref, var_ref, k_ref, cnt_ref,
    up_ref, dn_ref, own_ref, edge_ref,
):
    cls = cls_ref[...]
    kc = jnp.zeros(cls.shape, F32)
    for index in range(12):
        kc = jnp.where(cls == index, k_ref[index], kc)
    own_ref[pl.ds(PAD, CELLS), :] = kc
    up_ref[pl.ds(MSG_KC, CELLS), :] = kc
    dn_ref[pl.ds(MSG_KC, CELLS), :] = kc
    kedge = edge_pack(
        lambda l, r: None
        if l == LEV
        else jnp.broadcast_to(kc[l * ROWS + r : l * ROWS + r + 1, :], (8, COLS))
    )
    edge_ref[pl.ds(MEM, 8), :] = kedge
    own_ref[pl.ds(MEM, 8), :] = kedge
    up_ref[pl.ds(MSG_EDGE + MEM, 8), :] = kedge
    dn_ref[pl.ds(MSG_EDGE + MEM, 8), :] = kedge

    own_ref[pl.ds(PAD + CELLS, 2 * CELLS), :] = scatter_obs(
        idx_ref, val_ref, var_ref, cnt_ref[0]
    )
    for g in range(GROUPS):
        h = {}
        for l in range(LEV):
            for r in range(ROWS):
                block = h_ref[pl.ds(g * 8 * CELLS + l * ROWS + r, 8, stride=CELLS), :]
                h[l, r] = block
                if r < HALO:
                    up_ref[pl.ds((l * HALO + r) * MEM + g * 8, 8), :] = block
                if r >= ROWS - HALO:
                    dn_ref[pl.ds((l * HALO + r - 1) * MEM + g * 8, 8), :] = block
        for r in range(ROWS):
            block = f_ref[pl.ds(g * 8 * ROWS + r, 8, stride=ROWS), :]
            h[LEV, r] = block
            if r < 2:
                up_ref[pl.ds(MSG_FORCE + r * MEM + g * 8, 8), :] = block
            else:
                dn_ref[pl.ds(MSG_FORCE + (r - 2) * MEM + g * 8, 8), :] = block
        edge = edge_pack(lambda l, r: h[l, r])
        edge_ref[pl.ds(g * 8, 8), :] = edge
        own_ref[pl.ds(g * 8, 8), :] = edge
        up_ref[pl.ds(MSG_EDGE + g * 8, 8), :] = edge
        dn_ref[pl.ds(MSG_EDGE + g * 8, 8), :] = edge


def forecast_kernel(
    regions, tiles,
    h_ref, f_ref, own_ref, above_ref, below_ref, el_ref, er_ref,
    uel_ref, uer_ref, del_ref, der_ref,
    dev_ref, mean_ref, pay_ref,
    z_ref, ks_ref, kr_ref, face_ref, hold_ref, gram_ref,
):
    ri = lax.axis_index("region")
    ti = lax.axis_index("tile")
    top_ok = jnp.where(ri > 0, 1.0, 0.0)
    bot_ok = jnp.where(ri < regions - 1, 1.0, 0.0)
    left_ok = jnp.where(ti > 0, 1.0, 0.0)
    right_ok = jnp.where(ti < tiles - 1, 1.0, 0.0)
    lane = lanes()
    half = lane % 64
    srow = half // 6
    scol = half % 6
    is_left = lane < 64
    row_ok = jnp.where(srow < HALO, top_ok, jnp.where(srow >= HALO + ROWS, bot_ok, 1.0))
    side_ok = jnp.where(
        is_left, jnp.where(scol < 3, left_ok, 1.0), jnp.where(scol >= 3, right_ok, 1.0)
    )
    smask = jnp.where(half < 60, row_ok * side_ok, 0.0)
    low_k = lane % 6 < 3

    def strips(base):
        own, left, right = base(own_ref, 0), base(el_ref, 0), base(er_ref, 0)
        uown, ul, ur = base(above_ref, MSG_EDGE), base(uel_ref, 0), base(uer_ref, 0)
        down, dl, dr = base(below_ref, MSG_EDGE), base(del_ref, 0), base(der_ref, 0)
        parts = (
            (jnp.where(low_k, ul, uown), jnp.where(low_k, uown, ur), -1),
            (jnp.where(low_k, left, own), jnp.where(low_k, own, right), 3),
            (jnp.where(low_k, dl, down), jnp.where(low_k, down, dr), 7),
        )
        out = []
        for l in range(LEV + 1):
            strip = jnp.zeros((8, COLS), F32)
            for lo, hi, first in parts:
                inside = (srow >= first) & (srow < first + ROWS)
                strip = jnp.where(inside & is_left, roll(lo, first * 6 - l * 24), strip)
                strip = jnp.where(inside & ~is_left, roll(hi, 64 + first * 6 - l * 24), strip)
            out.append(strip * smask)
        return out

    kstrip = strips(lambda ref, base: ref[pl.ds(base + MEM, 8), :])
    def kc_row(l, e):
        r = e - HALO
        if r < 0:
            at = MSG_KC + l * ROWS + r + ROWS
            return above_ref[at : at + 1, :] * top_ok
        if r >= ROWS:
            at = MSG_KC + l * ROWS + r - ROWS
            return below_ref[at : at + 1, :] * bot_ok
        at = PAD + l * ROWS + r
        return own_ref[at : at + 1, :]

    for l in range(LEV):
        ks_ref[pl.ds(l * 8, 8), :] = 0.0625 * kstrip[l]
        for e in range(EXT):
            kr_ref[pl.ds((l * EXT + e) * 8, 8), :] = jnp.broadcast_to(
                0.0625 * kc_row(l, e), (8, COLS)
            )

    def conduct(kc, h):
        return kc * (2.0 + jnp.tanh(0.5 * h))

    joint = is_left & (scol == 1)

    def group(g, carry):
        base = g * 8

        def prior_row(l, e):
            r = e - HALO
            if r < 0:
                at = (l * HALO + r + HALO) * MEM
                return above_ref[pl.ds(at + base, 8), :] * top_ok
            if r >= ROWS:
                at = (l * HALO + r - ROWS) * MEM
                return below_ref[pl.ds(at + base, 8), :] * bot_ok
            return h_ref[pl.ds(g * (8 * CELLS) + l * ROWS + r, 8, stride=CELLS), :]

        def force_row(e):
            r = e - HALO
            if r < 0:
                return above_ref[pl.ds(MSG_FORCE + (r + 2) * MEM + base, 8), :]
            if r >= ROWS:
                return below_ref[pl.ds(MSG_FORCE + (r - ROWS) * MEM + base, 8), :]
            return f_ref[pl.ds(g * (8 * ROWS) + r, 8, stride=ROWS), :]

        hs = strips(lambda ref, first: ref[pl.ds(first + base, 8), :])
        fs = hs[LEV]
        for step in range(STEPS):
            sk = [conduct(ks_ref[pl.ds(l * 8, 8), :], hs[l]) for l in range(LEV)]
            faces = [
                (sk[l] + roll(sk[l], -1)) * (roll(hs[l], -1) - hs[l]) for l in range(LEV)
            ]
            for l in range(LEV):
                edge = jnp.where(joint, roll(faces[l], -65), faces[l])
                face_ref[pl.ds((step * LEV + l) * 8, 8), :] = edge
            if step == STEPS - 1:
                break
            fresh = []
            last = None
            for l in range(LEV):
                down = (sk[l] + roll(sk[l], -6)) * (roll(hs[l], -6) - hs[l])
                flux = (faces[l] - roll(faces[l], 1)) + (down - roll(down, 6))
                if l > 0:
                    flux = flux - last
                if l < LEV - 1:
                    last = 0.5 * (sk[l] + sk[l + 1]) * (hs[l + 1] - hs[l])
                    flux = flux + last
                if l == 0:
                    flux = flux + 0.25 * fs
                fresh.append((hs[l] + flux) * smask)
            hs = fresh

        for step in range(STEPS):
            def row(l, e):
                if step == 0:
                    return prior_row(l, e)
                return hold_ref[step - 1, pl.ds((l * EXT + e) * 8, 8), :]

            h_now = k_now = face_now = None
            for e in range(step, EXT - step):
                h_new = [row(l, e) for l in range(LEV)]
                k_new = [
                    conduct(kr_ref[pl.ds((l * EXT + e) * 8, 8), :], h_new[l])
                    for l in range(LEV)
                ]
                face_new = None
                if e > step:
                    face_new = [
                        (k_now[l] + k_new[l]) * (h_new[l] - h_now[l]) for l in range(LEV)
                    ]
                if e > step + 1:
                    at = e - 1
                    r = at - HALO
                    last = None
                    for l in range(LEV):
                        here, kh = h_now[l], k_now[l]
                        edge = roll(
                            face_ref[pl.ds((step * LEV + l) * 8, 8), :], -(at * 6 + 2)
                        )
                        face = (kh + roll(kh, -1)) * (roll(here, -1) - here)
                        face = jnp.where(lane == COLS - 1, edge, face)
                        behind = jnp.where(lane == 0, edge, roll(face, 1))
                        flux = (face - behind) + (face_new[l] - face_now[l])
                        if l > 0:
                            flux = flux - last
                        if l < LEV - 1:
                            last = 0.5 * (kh + k_now[l + 1]) * (h_now[l + 1] - here)
                            flux = flux + last
                        if l == 0:
                            flux = flux + 0.25 * force_row(at)
                        value = here + flux
                        if step == STEPS - 1:
                            lr = l * ROWS + r
                            dev_ref[pl.ds(base, 8), lr * COLS : (lr + 1) * COLS] = value
                            continue
                        if r < 0:
                            value = value * top_ok
                        elif r >= ROWS:
                            value = value * bot_ok
                        hold_ref[step, pl.ds((l * EXT + at) * 8, 8), :] = value
                h_now, k_now, face_now = h_new, k_new, face_new
        return carry

    lax.fori_loop(0, GROUPS, group, 0)

    for lr in range(CELLS):
        cols = slice(lr * COLS, (lr + 1) * COLS)
        head = dev_ref[:, cols]
        mean = jnp.sum(head, axis=0, keepdims=True) * (1.0 / MEM)
        mean_ref[lr : lr + 1, :] = mean
        dev = head - mean
        dev_ref[:, cols] = dev
        scale = own_ref[PAD + CELLS + lr : PAD + CELLS + lr + 1, :]
        z_ref[0:MEM, cols] = dev * scale
        rest = own_ref[PAD + 2 * CELLS + lr : PAD + 2 * CELLS + lr + 1, :] - scale * mean
        z_ref[MEM : MEM + 8, cols] = jnp.broadcast_to(rest, (8, COLS))
    gram_ref[:, 0:MEM] = lax.dot_general(
        z_ref[...], dev_ref[...], (((1,), (1,)), ((), ())),
        precision=HIGHEST, preferred_element_type=F32,
    )
    gram_ref[:, MEM:COLS] = jnp.zeros((PAD, COLS - MEM), F32)

    vec = gram_ref[MEM:PAD, :]
    sub = lax.broadcasted_iota(jnp.int32, (8, COLS), 0)

    def stripe(i):
        block = gram_ref[8 * i : 8 * i + 8, :]
        block = jnp.where((sub == 7) & (lane >= 8 * i) & (lane < 8 * i + 7), vec, block)
        return jnp.where((sub == 6) & (lane == 8 * i + 5), roll(vec, -2), block)

    def joined(i):
        if i == 0:
            return stripe(0)
        return jnp.where(lane >= 8 * i, stripe(i), roll(stripe(8 - i), 8 * i - MEM))

    first = jnp.where(lane < MEM, joined(0), roll(joined(1), MEM))
    second = jnp.where(lane < MEM, joined(2), roll(joined(3), MEM))
    middle = stripe(4)
    third = roll(middle, -32)[0:2]
    for q in range(1, 4):
        third = jnp.where(
            lane[0:2] >= 32 * q, roll(middle, 32 * q - 32)[2 * q : 2 * q + 2], third
        )
    pieces = [block[2 * q : 2 * q + 2] for block in (first, second) for q in range(4)]
    for i, piece in enumerate(pieces + [third]):
        for c in range(regions):
            pay_ref[c, :, i * COLS : (i + 1) * COLS] = piece


def analysis_kernel(copies, pay_ref, dev_ref, mean_ref, out_ref, m_ref):
    lane = lanes()
    sub = lax.broadcasted_iota(jnp.int32, (8, COLS), 0)
    total = pay_ref[0]
    for c in range(1, copies):
        total = total + pay_ref[c]
    piece = [total[:, i * COLS : (i + 1) * COLS] for i in range(9)]
    first = jnp.concatenate(piece[0:4], axis=0)
    second = jnp.concatenate(piece[4:8], axis=0)
    halves = [
        first,
        roll(first, MEM),
        second,
        roll(second, MEM),
        jnp.concatenate([roll(piece[8], 32 - 32 * q) for q in range(4)], axis=0),
    ]
    bvec = jnp.zeros((1, COLS), F32)
    for i in range(8):
        block = halves[i] if i <= 4 else roll(halves[8 - i], MEM - 8 * (8 - i))
        here = lane[0:1] // 8 == i
        tail = jnp.where(lane[0:1] % 8 == 7, roll(block, 2)[6:7], block[7:8])
        bvec = jnp.where(here, tail, bvec)
        keep = (lane >= sub + 8 * i) & (lane < MEM)
        block = jnp.where(keep, block, 0.0)
        block = block + jnp.where(lane == sub + 8 * i, MEM - 1.0, 0.0)
        block = block + jnp.where(lane == sub + (8 * i + MEM), 1.0, 0.0)
        m_ref[8 * i : 8 * i + 8, :] = block
    bvec = roll(bvec, MEM)

    for kb in range(8):
        block = m_ref[8 * kb : 8 * kb + 8, :]
        at = 8 * kb
        full = {
            (i, j): jnp.broadcast_to(block[j : j + 1, at + i : at + i + 1], (8, COLS))
            for i in range(8)
            for j in range(i + 1)
        }
        for j in range(8):
            inv = lax.rsqrt(full[j, j])
            low = {i: full[i, j] * inv for i in range(j + 1, 8)}
            for i in range(j + 1, 8):
                for m in range(j + 1, i + 1):
                    full[i, m] = full[i, m] - low[i] * low[m]
            prow = jnp.broadcast_to(block[j : j + 1, :], (8, COLS)) * inv
            column = jnp.zeros((8, COLS), F32)
            for i in range(j + 1, 8):
                column = jnp.where(sub == i, low[i], column)
            block = jnp.where(sub == j, prow, block - column * prow)
        m_ref[8 * kb : 8 * kb + 8, :] = block
        if kb < 7:
            later = 8 * (kb + 1)
            update = lax.dot_general(
                block[:, 0:MEM], block, (((0,), (0,)), ((), ())),
                precision=HIGHEST, preferred_element_type=F32,
            )
            m_ref[later:MEM, :] = m_ref[later:MEM, :] - update[later:MEM, :]

    inverse = m_ref[...]
    bvec = jnp.where(lane[0:1] >= MEM, bvec, 0.0)
    y = jnp.sum(inverse * bvec, axis=1, keepdims=True)
    w = jnp.sum(inverse * y, axis=0, keepdims=True)
    blend = (inverse * jnp.sqrt(jnp.full((1, COLS), MEM - 1.0, F32)) + w)[:, MEM:COLS]
    for lr in range(CELLS):
        cols = slice(lr * COLS, (lr + 1) * COLS)
        value = mean_ref[lr : lr + 1, :] + jnp.dot(
            blend, dev_ref[:, cols], precision=HIGHEST, preferred_element_type=F32
        )
        out_ref[pl.ds(lr, MEM, stride=CELLS), :] = value


def vmem():
    return pl.BlockSpec(memory_space=pltpu.VMEM)


def smem():
    return pl.BlockSpec(memory_space=pltpu.SMEM)


PARAMS = pltpu.CompilerParams(vmem_limit_bytes=32 * 1024 * 1024)


def shift(x, axis, by, wrap=True):
    count = lax.axis_size(axis)
    pairs = [(i, (i + by) % count) for i in range(count) if wrap or 0 <= i + by < count]
    return lax.ppermute(x, axis, pairs)


def shards(prior, source, soil_class, soil_k, obs_index, obs_value, obs_var, obs_count):
    regions, tiles = lax.axis_size("region"), lax.axis_size("tile")
    prior = prior.reshape(MEM * CELLS, COLS)
    source = source.reshape(MEM * ROWS, COLS)
    soil_class = soil_class.reshape(CELLS, COLS)
    slots = obs_index.shape[0]

    def out(*shape):
        return jax.ShapeDtypeStruct(shape, F32)

    up, dn, own, edge = pl.pallas_call(
        pack_kernel,
        out_shape=(
            out(MSG_ROWS, COLS), out(MSG_ROWS, COLS), out(PAD + 3 * CELLS, COLS), out(PAD, COLS)
        ),
        in_specs=[vmem()] * 6 + [smem()] * 2,
        out_specs=(vmem(),) * 4,
        compiler_params=PARAMS,
        name="pack",
    )(
        prior, source, soil_class,
        obs_index.reshape(1, slots), obs_value.reshape(1, slots), obs_var.reshape(1, slots),
        soil_k, obs_count,
    )
    above = shift(dn, "region", 1)
    below = shift(up, "region", -1)
    el = shift(edge, "tile", 1, False)
    er = shift(edge, "tile", -1, False)
    uel, uer = shift(el, "region", 1), shift(er, "region", 1)
    bel, ber = shift(el, "region", -1), shift(er, "region", -1)
    dev, mean, pay = pl.pallas_call(
        functools.partial(forecast_kernel, regions, tiles),
        out_shape=(out(MEM, CELLS * COLS), out(CELLS, COLS), out(regions, 2, PAYLOAD)),
        in_specs=[vmem()] * 11,
        out_specs=(vmem(),) * 3,
        scratch_shapes=[
            pltpu.VMEM((PAD, CELLS * COLS), F32),
            pltpu.VMEM((LEV * 8, COLS), F32),
            pltpu.VMEM((LEV * EXT * 8, COLS), F32),
            pltpu.VMEM((STEPS * LEV * 8, COLS), F32),
            pltpu.VMEM((STEPS - 1, LEV * EXT * 8, COLS), F32),
            pltpu.VMEM((PAD, COLS), F32),
        ],
        compiler_params=PARAMS,
        name="forecast",
    )(prior, source, own, above, below, el, er, uel, uer, bel, ber)
    part = lax.all_to_all(pay, "region", 0, 0).sum(axis=0)
    pay = lax.all_to_all(jnp.broadcast_to(part, (tiles,) + part.shape), "tile", 0, 0)
    result = pl.pallas_call(
        functools.partial(analysis_kernel, tiles),
        out_shape=out(MEM * CELLS, COLS),
        in_specs=[vmem()] * 3,
        out_specs=vmem(),
        scratch_shapes=[pltpu.VMEM((MEM, COLS), F32)],
        compiler_params=PARAMS,
        name="analysis",
    )(pay, dev, mean)
    return result.reshape(MEM, LEV, ROWS, COLS)


def solution(mesh):
    return jax.shard_map(
        shards,
        mesh=mesh,
        in_specs=(
            P(None, None, "region", "tile"),
            P(None, "region", "tile"),
            P(None, "region", "tile"),
            P(),
            P(("region", "tile")),
            P(("region", "tile")),
            P(("region", "tile")),
            P(("region", "tile")),
        ),
        out_specs=P(None, None, "region", "tile"),
        check_vma=False,
    )
```

```python
import functools

import jax
import jax.numpy as jnp
from jax import lax
from jax.experimental import pallas as pl
from jax.experimental.pallas import tpu as pltpu
from jax.sharding import PartitionSpec as P

STEPS = 3
MEM = 64
LEV = 4
ROWS = 4
COLS = 128
GROUPS = MEM // 8
CELLS = LEV * ROWS
HALO = 3
EXT = ROWS + 2 * HALO
PAD = 72
MSG_FORCE = LEV * HALO * MEM
MSG_KC = MSG_FORCE + 2 * MEM
MSG_EDGE = MSG_KC + CELLS
MSG_ROWS = MSG_EDGE + PAD
PAYLOAD = 9 * COLS
HIGHEST = lax.Precision.HIGHEST
F32 = jnp.float32


def roll(x, shift):
    shift = shift % COLS
    return x if shift == 0 else pltpu.roll(x, shift, 1)


def lanes(rows=8):
    return lax.broadcasted_iota(jnp.int32, (rows, COLS), 1)


def edge_pack(rows_of):
    lane = lanes()
    out = jnp.zeros((8, COLS), F32)
    for l in range(LEV + 1):
        for r in range(ROWS):
            block = rows_of(l, r)
            if block is None:
                continue
            start = l * 24 + r * 6
            out = jnp.where((lane >= start) & (lane < start + 6), roll(block, 3 + start), out)
    return out


def scatter_obs(idx_ref, val_ref, var_ref, count):
    slots = idx_ref.shape[1]
    idx = idx_ref[...]
    slot = lax.broadcasted_iota(jnp.int32, (1, slots), 1)
    weight = jnp.where(slot < count, 1.0 / var_ref[...], 0.0)
    place = lax.broadcasted_iota(jnp.int32, (CELLS, slots), 0) == idx // COLS
    lhs = jnp.concatenate(
        [jnp.where(place, weight, 0.0), jnp.where(place, weight * val_ref[...], 0.0)], axis=0
    )
    rhs = jnp.where(
        lax.broadcasted_iota(jnp.int32, (COLS, slots), 0) == idx % COLS, 1.0, 0.0
    )
    return lax.dot_general(
        lhs, rhs, (((1,), (1,)), ((), ())), precision=HIGHEST, preferred_element_type=F32
    )


def pack_kernel(
    h_ref, f_ref, cls_ref, idx_ref, val_ref, var_ref, k_ref, cnt_ref,
    up_ref, dn_ref, own_ref, edge_ref,
):
    cls = cls_ref[...]
    kc = jnp.zeros(cls.shape, F32)
    for index in range(12):
        kc = jnp.where(cls == index, k_ref[index], kc)
    own_ref[pl.ds(PAD, CELLS), :] = kc
    up_ref[pl.ds(MSG_KC, CELLS), :] = kc
    dn_ref[pl.ds(MSG_KC, CELLS), :] = kc
    kedge = edge_pack(
        lambda l, r: None
        if l == LEV
        else jnp.broadcast_to(kc[l * ROWS + r : l * ROWS + r + 1, :], (8, COLS))
    )
    edge_ref[pl.ds(MEM, 8), :] = kedge
    own_ref[pl.ds(MEM, 8), :] = kedge
    up_ref[pl.ds(MSG_EDGE + MEM, 8), :] = kedge
    dn_ref[pl.ds(MSG_EDGE + MEM, 8), :] = kedge

    own_ref[pl.ds(PAD + CELLS, 2 * CELLS), :] = scatter_obs(
        idx_ref, val_ref, var_ref, cnt_ref[0]
    )
    for g in range(GROUPS):
        h = {}
        for l in range(LEV):
            for r in range(ROWS):
                block = h_ref[pl.ds(g * 8 * CELLS + l * ROWS + r, 8, stride=CELLS), :]
                h[l, r] = block
                if r < HALO:
                    up_ref[pl.ds((l * HALO + r) * MEM + g * 8, 8), :] = block
                if r >= ROWS - HALO:
                    dn_ref[pl.ds((l * HALO + r - 1) * MEM + g * 8, 8), :] = block
        for r in range(ROWS):
            block = f_ref[pl.ds(g * 8 * ROWS + r, 8, stride=ROWS), :]
            h[LEV, r] = block
            if r < 2:
                up_ref[pl.ds(MSG_FORCE + r * MEM + g * 8, 8), :] = block
            else:
                dn_ref[pl.ds(MSG_FORCE + (r - 2) * MEM + g * 8, 8), :] = block
        edge = edge_pack(lambda l, r: h[l, r])
        edge_ref[pl.ds(g * 8, 8), :] = edge
        own_ref[pl.ds(g * 8, 8), :] = edge
        up_ref[pl.ds(MSG_EDGE + g * 8, 8), :] = edge
        dn_ref[pl.ds(MSG_EDGE + g * 8, 8), :] = edge


def forecast_kernel(
    regions, tiles,
    h_ref, f_ref, own_ref, above_ref, below_ref, el_ref, er_ref,
    uel_ref, uer_ref, del_ref, der_ref,
    dev_ref, mean_ref, pay_ref,
    z_ref, ks_ref, kr_ref, face_ref, hold_ref, gram_ref,
):
    ri = lax.axis_index("region")
    ti = lax.axis_index("tile")
    top_ok = jnp.where(ri > 0, 1.0, 0.0)
    bot_ok = jnp.where(ri < regions - 1, 1.0, 0.0)
    left_ok = jnp.where(ti > 0, 1.0, 0.0)
    right_ok = jnp.where(ti < tiles - 1, 1.0, 0.0)
    lane = lanes()
    half = lane % 64
    srow = half // 6
    scol = half % 6
    is_left = lane < 64
    row_ok = jnp.where(srow < HALO, top_ok, jnp.where(srow >= HALO + ROWS, bot_ok, 1.0))
    side_ok = jnp.where(
        is_left, jnp.where(scol < 3, left_ok, 1.0), jnp.where(scol >= 3, right_ok, 1.0)
    )
    smask = jnp.where(half < 60, row_ok * side_ok, 0.0)
    low_k = lane % 6 < 3

    def strips(base):
        own, left, right = base(own_ref, 0), base(el_ref, 0), base(er_ref, 0)
        uown, ul, ur = base(above_ref, MSG_EDGE), base(uel_ref, 0), base(uer_ref, 0)
        down, dl, dr = base(below_ref, MSG_EDGE), base(del_ref, 0), base(der_ref, 0)
        parts = (
            (jnp.where(low_k, ul, uown), jnp.where(low_k, uown, ur), -1),
            (jnp.where(low_k, left, own), jnp.where(low_k, own, right), 3),
            (jnp.where(low_k, dl, down), jnp.where(low_k, down, dr), 7),
        )
        out = []
        for l in range(LEV + 1):
            strip = jnp.zeros((8, COLS), F32)
            for lo, hi, first in parts:
                inside = (srow >= first) & (srow < first + ROWS)
                strip = jnp.where(inside & is_left, roll(lo, first * 6 - l * 24), strip)
                strip = jnp.where(inside & ~is_left, roll(hi, 64 + first * 6 - l * 24), strip)
            out.append(strip * smask)
        return out

    kstrip = strips(lambda ref, base: ref[pl.ds(base + MEM, 8), :])
    def kc_row(l, e):
        r = e - HALO
        if r < 0:
            at = MSG_KC + l * ROWS + r + ROWS
            return above_ref[at : at + 1, :] * top_ok
        if r >= ROWS:
            at = MSG_KC + l * ROWS + r - ROWS
            return below_ref[at : at + 1, :] * bot_ok
        at = PAD + l * ROWS + r
        return own_ref[at : at + 1, :]

    for l in range(LEV):
        ks_ref[pl.ds(l * 8, 8), :] = 0.0625 * kstrip[l]
        for e in range(EXT):
            kr_ref[pl.ds((l * EXT + e) * 8, 8), :] = jnp.broadcast_to(
                0.0625 * kc_row(l, e), (8, COLS)
            )

    def conduct(kc, h):
        return kc * (2.0 + jnp.tanh(0.5 * h))

    joint = is_left & (scol == 1)

    def group(g, carry):
        base = g * 8

        def prior_row(l, e):
            r = e - HALO
            if r < 0:
                at = (l * HALO + r + HALO) * MEM
                return above_ref[pl.ds(at + base, 8), :] * top_ok
            if r >= ROWS:
                at = (l * HALO + r - ROWS) * MEM
                return below_ref[pl.ds(at + base, 8), :] * bot_ok
            return h_ref[pl.ds(g * (8 * CELLS) + l * ROWS + r, 8, stride=CELLS), :]

        def force_row(e):
            r = e - HALO
            if r < 0:
                return above_ref[pl.ds(MSG_FORCE + (r + 2) * MEM + base, 8), :]
            if r >= ROWS:
                return below_ref[pl.ds(MSG_FORCE + (r - ROWS) * MEM + base, 8), :]
            return f_ref[pl.ds(g * (8 * ROWS) + r, 8, stride=ROWS), :]

        hs = strips(lambda ref, first: ref[pl.ds(first + base, 8), :])
        fs = hs[LEV]
        for step in range(STEPS):
            sk = [conduct(ks_ref[pl.ds(l * 8, 8), :], hs[l]) for l in range(LEV)]
            faces = [
                (sk[l] + roll(sk[l], -1)) * (roll(hs[l], -1) - hs[l]) for l in range(LEV)
            ]
            for l in range(LEV):
                edge = jnp.where(joint, roll(faces[l], -65), faces[l])
                face_ref[pl.ds((step * LEV + l) * 8, 8), :] = edge
            if step == STEPS - 1:
                break
            fresh = []
            last = None
            for l in range(LEV):
                down = (sk[l] + roll(sk[l], -6)) * (roll(hs[l], -6) - hs[l])
                flux = (faces[l] - roll(faces[l], 1)) + (down - roll(down, 6))
                if l > 0:
                    flux = flux - last
                if l < LEV - 1:
                    last = 0.5 * (sk[l] + sk[l + 1]) * (hs[l + 1] - hs[l])
                    flux = flux + last
                if l == 0:
                    flux = flux + 0.25 * fs
                fresh.append((hs[l] + flux) * smask)
            hs = fresh

        for step in range(STEPS):
            def row(l, e):
                if step == 0:
                    return prior_row(l, e)
                return hold_ref[step - 1, pl.ds((l * EXT + e) * 8, 8), :]

            h_now = k_now = face_now = None
            for e in range(step, EXT - step):
                h_new = [row(l, e) for l in range(LEV)]
                k_new = [
                    conduct(kr_ref[pl.ds((l * EXT + e) * 8, 8), :], h_new[l])
                    for l in range(LEV)
                ]
                face_new = None
                if e > step:
                    face_new = [
                        (k_now[l] + k_new[l]) * (h_new[l] - h_now[l]) for l in range(LEV)
                    ]
                if e > step + 1:
                    at = e - 1
                    r = at - HALO
                    last = None
                    for l in range(LEV):
                        here, kh = h_now[l], k_now[l]
                        edge = roll(
                            face_ref[pl.ds((step * LEV + l) * 8, 8), :], -(at * 6 + 2)
                        )
                        face = (kh + roll(kh, -1)) * (roll(here, -1) - here)
                        face = jnp.where(lane == COLS - 1, edge, face)
                        behind = jnp.where(lane == 0, edge, roll(face, 1))
                        flux = (face - behind) + (face_new[l] - face_now[l])
                        if l > 0:
                            flux = flux - last
                        if l < LEV - 1:
                            last = 0.5 * (kh + k_now[l + 1]) * (h_now[l + 1] - here)
                            flux = flux + last
                        if l == 0:
                            flux = flux + 0.25 * force_row(at)
                        value = here + flux
                        if step == STEPS - 1:
                            lr = l * ROWS + r
                            dev_ref[pl.ds(base, 8), lr * COLS : (lr + 1) * COLS] = value
                            continue
                        if r < 0:
                            value = value * top_ok
                        elif r >= ROWS:
                            value = value * bot_ok
                        hold_ref[step, pl.ds((l * EXT + at) * 8, 8), :] = value
                h_now, k_now, face_now = h_new, k_new, face_new
        return carry

    lax.fori_loop(0, GROUPS, group, 0)

    for lr in range(CELLS):
        cols = slice(lr * COLS, (lr + 1) * COLS)
        head = dev_ref[:, cols]
        mean = jnp.sum(head, axis=0, keepdims=True) * (1.0 / MEM)
        mean_ref[lr : lr + 1, :] = mean
        dev = head - mean
        dev_ref[:, cols] = dev
        scale = own_ref[PAD + CELLS + lr : PAD + CELLS + lr + 1, :]
        z_ref[0:MEM, cols] = dev * scale
        rest = own_ref[PAD + 2 * CELLS + lr : PAD + 2 * CELLS + lr + 1, :] - scale * mean
        z_ref[MEM : MEM + 8, cols] = jnp.broadcast_to(rest, (8, COLS))
    gram_ref[:, 0:MEM] = lax.dot_general(
        z_ref[...], dev_ref[...], (((1,), (1,)), ((), ())),
        precision=HIGHEST, preferred_element_type=F32,
    )
    gram_ref[:, MEM:COLS] = jnp.zeros((PAD, COLS - MEM), F32)

    vec = gram_ref[MEM:PAD, :]
    sub = lax.broadcasted_iota(jnp.int32, (8, COLS), 0)

    def stripe(i):
        block = gram_ref[8 * i : 8 * i + 8, :]
        block = jnp.where((sub == 7) & (lane >= 8 * i) & (lane < 8 * i + 7), vec, block)
        return jnp.where((sub == 6) & (lane == 8 * i + 5), roll(vec, -2), block)

    def joined(i):
        if i == 0:
            return stripe(0)
        return jnp.where(lane >= 8 * i, stripe(i), roll(stripe(8 - i), 8 * i - MEM))

    first = jnp.where(lane < MEM, joined(0), roll(joined(1), MEM))
    second = jnp.where(lane < MEM, joined(2), roll(joined(3), MEM))
    middle = stripe(4)
    third = roll(middle, -32)[0:2]
    for q in range(1, 4):
        third = jnp.where(
            lane[0:2] >= 32 * q, roll(middle, 32 * q - 32)[2 * q : 2 * q + 2], third
        )
    pieces = [block[2 * q : 2 * q + 2] for block in (first, second) for q in range(4)]
    for i, piece in enumerate(pieces + [third]):
        for c in range(tiles):
            pay_ref[c, :, i * COLS : (i + 1) * COLS] = piece


def analysis_kernel(copies, pay_ref, dev_ref, mean_ref, out_ref, m_ref):
    lane = lanes()
    sub = lax.broadcasted_iota(jnp.int32, (8, COLS), 0)
    total = pay_ref[0]
    for c in range(1, copies):
        total = total + pay_ref[c]
    piece = [total[:, i * COLS : (i + 1) * COLS] for i in range(9)]
    first = jnp.concatenate(piece[0:4], axis=0)
    second = jnp.concatenate(piece[4:8], axis=0)
    halves = [
        first,
        roll(first, MEM),
        second,
        roll(second, MEM),
        jnp.concatenate([roll(piece[8], 32 - 32 * q) for q in range(4)], axis=0),
    ]
    bvec = jnp.zeros((1, COLS), F32)
    for i in range(8):
        block = halves[i] if i <= 4 else roll(halves[8 - i], MEM - 8 * (8 - i))
        here = lane[0:1] // 8 == i
        tail = jnp.where(lane[0:1] % 8 == 7, roll(block, 2)[6:7], block[7:8])
        bvec = jnp.where(here, tail, bvec)
        keep = (lane >= sub + 8 * i) & (lane < MEM)
        block = jnp.where(keep, block, 0.0)
        block = block + jnp.where(lane == sub + 8 * i, MEM - 1.0, 0.0)
        block = block + jnp.where(lane == sub + (8 * i + MEM), 1.0, 0.0)
        m_ref[8 * i : 8 * i + 8, :] = block
    bvec = roll(bvec, MEM)

    for kb in range(8):
        block = m_ref[8 * kb : 8 * kb + 8, :]
        at = 8 * kb
        full = {
            (i, j): jnp.broadcast_to(block[j : j + 1, at + i : at + i + 1], (8, COLS))
            for i in range(8)
            for j in range(i + 1)
        }
        for j in range(8):
            inv = lax.rsqrt(full[j, j])
            low = {i: full[i, j] * inv for i in range(j + 1, 8)}
            for i in range(j + 1, 8):
                for m in range(j + 1, i + 1):
                    full[i, m] = full[i, m] - low[i] * low[m]
            prow = jnp.broadcast_to(block[j : j + 1, :], (8, COLS)) * inv
            column = jnp.zeros((8, COLS), F32)
            for i in range(j + 1, 8):
                column = jnp.where(sub == i, low[i], column)
            block = jnp.where(sub == j, prow, block - column * prow)
        m_ref[8 * kb : 8 * kb + 8, :] = block
        if kb < 7:
            later = 8 * (kb + 1)
            update = lax.dot_general(
                block[:, 0:MEM], block, (((0,), (0,)), ((), ())),
                precision=HIGHEST, preferred_element_type=F32,
            )
            m_ref[later:MEM, :] = m_ref[later:MEM, :] - update[later:MEM, :]

    inverse = m_ref[...]
    bvec = jnp.where(lane[0:1] >= MEM, bvec, 0.0)
    y = jnp.sum(inverse * bvec, axis=1, keepdims=True)
    w = jnp.sum(inverse * y, axis=0, keepdims=True)
    blend = (inverse * jnp.sqrt(jnp.full((1, COLS), MEM - 1.0, F32)) + w)[:, MEM:COLS]
    for lr in range(CELLS):
        cols = slice(lr * COLS, (lr + 1) * COLS)
        value = mean_ref[lr : lr + 1, :] + jnp.dot(
            blend, dev_ref[:, cols], precision=HIGHEST, preferred_element_type=F32
        )
        out_ref[pl.ds(lr, MEM, stride=CELLS), :] = value


def vmem():
    return pl.BlockSpec(memory_space=pltpu.VMEM)


def smem():
    return pl.BlockSpec(memory_space=pltpu.SMEM)


PARAMS = pltpu.CompilerParams(vmem_limit_bytes=32 * 1024 * 1024)


def shift(x, axis, by, wrap=True):
    count = lax.axis_size(axis)
    pairs = [(i, (i + by) % count) for i in range(count) if wrap or 0 <= i + by < count]
    return lax.ppermute(x, axis, pairs)


def shards(prior, source, soil_class, soil_k, obs_index, obs_value, obs_var, obs_count):
    regions, tiles = lax.axis_size("region"), lax.axis_size("tile")
    prior = prior.reshape(MEM * CELLS, COLS)
    source = source.reshape(MEM * ROWS, COLS)
    soil_class = soil_class.reshape(CELLS, COLS)
    slots = obs_index.shape[0]

    def out(*shape):
        return jax.ShapeDtypeStruct(shape, F32)

    up, dn, own, edge = pl.pallas_call(
        pack_kernel,
        out_shape=(
            out(MSG_ROWS, COLS), out(MSG_ROWS, COLS), out(PAD + 3 * CELLS, COLS), out(PAD, COLS)
        ),
        in_specs=[vmem()] * 6 + [smem()] * 2,
        out_specs=(vmem(),) * 4,
        compiler_params=PARAMS,
        name="pack",
    )(
        prior, source, soil_class,
        obs_index.reshape(1, slots), obs_value.reshape(1, slots), obs_var.reshape(1, slots),
        soil_k, obs_count,
    )
    above = shift(dn, "region", 1)
    below = shift(up, "region", -1)
    el = shift(edge, "tile", 1, False)
    er = shift(edge, "tile", -1, False)
    uel, uer = shift(el, "region", 1), shift(er, "region", 1)
    bel, ber = shift(el, "region", -1), shift(er, "region", -1)
    dev, mean, pay = pl.pallas_call(
        functools.partial(forecast_kernel, regions, tiles),
        out_shape=(out(MEM, CELLS * COLS), out(CELLS, COLS), out(tiles, 2, PAYLOAD)),
        in_specs=[vmem()] * 11,
        out_specs=(vmem(),) * 3,
        scratch_shapes=[
            pltpu.VMEM((PAD, CELLS * COLS), F32),
            pltpu.VMEM((LEV * 8, COLS), F32),
            pltpu.VMEM((LEV * EXT * 8, COLS), F32),
            pltpu.VMEM((STEPS * LEV * 8, COLS), F32),
            pltpu.VMEM((STEPS - 1, LEV * EXT * 8, COLS), F32),
            pltpu.VMEM((PAD, COLS), F32),
        ],
        compiler_params=PARAMS,
        name="forecast",
    )(prior, source, own, above, below, el, er, uel, uer, bel, ber)
    part = lax.all_to_all(pay, "tile", 0, 0).sum(axis=0)
    pay = lax.all_to_all(jnp.broadcast_to(part, (regions,) + part.shape), "region", 0, 0)
    result = pl.pallas_call(
        functools.partial(analysis_kernel, regions),
        out_shape=out(MEM * CELLS, COLS),
        in_specs=[vmem()] * 3,
        out_specs=vmem(),
        scratch_shapes=[pltpu.VMEM((MEM, COLS), F32)],
        compiler_params=PARAMS,
        name="analysis",
    )(pay, dev, mean)
    return result.reshape(MEM, LEV, ROWS, COLS)


def solution(mesh):
    return jax.shard_map(
        shards,
        mesh=mesh,
        in_specs=(
            P(None, None, "region", "tile"),
            P(None, "region", "tile"),
            P(None, "region", "tile"),
            P(),
            P(("region", "tile")),
            P(("region", "tile")),
            P(("region", "tile")),
            P(("region", "tile")),
        ),
        out_specs=P(None, None, "region", "tile"),
        check_vma=False,
    )
```

```python
import functools

import jax
import jax.numpy as jnp
from jax import lax
from jax.experimental import pallas as pl
from jax.experimental.pallas import tpu as pltpu
from jax.sharding import PartitionSpec as P

STEPS = 3
MEM = 64
LEV = 4
ROWS = 4
COLS = 128
GROUPS = MEM // 8
CELLS = LEV * ROWS
HALO = 3
EXT = ROWS + 2 * HALO
PAD = 72
MSG_FORCE = LEV * HALO * MEM
MSG_KC = MSG_FORCE + 2 * MEM
MSG_EDGE = MSG_KC + CELLS
MSG_ROWS = MSG_EDGE + PAD
PAYLOAD = 9 * COLS
HIGHEST = lax.Precision.HIGHEST
F32 = jnp.float32


def roll(x, shift):
    shift = shift % COLS
    return x if shift == 0 else pltpu.roll(x, shift, 1)


def lanes(rows=8):
    return lax.broadcasted_iota(jnp.int32, (rows, COLS), 1)


def edge_pack(rows_of):
    lane = lanes()
    out = jnp.zeros((8, COLS), F32)
    for l in range(LEV + 1):
        for r in range(ROWS):
            block = rows_of(l, r)
            if block is None:
                continue
            start = l * 24 + r * 6
            out = jnp.where((lane >= start) & (lane < start + 6), roll(block, 3 + start), out)
    return out


def scatter_obs(idx_ref, val_ref, var_ref, count):
    slots = idx_ref.shape[1]
    idx = idx_ref[...]
    slot = lax.broadcasted_iota(jnp.int32, (1, slots), 1)
    weight = jnp.where(slot < count, 1.0 / var_ref[...], 0.0)
    place = lax.broadcasted_iota(jnp.int32, (CELLS, slots), 0) == idx // COLS
    lhs = jnp.concatenate(
        [jnp.where(place, weight, 0.0), jnp.where(place, weight * val_ref[...], 0.0)], axis=0
    )
    rhs = jnp.where(
        lax.broadcasted_iota(jnp.int32, (COLS, slots), 0) == idx % COLS, 1.0, 0.0
    )
    return lax.dot_general(
        lhs, rhs, (((1,), (1,)), ((), ())), precision=HIGHEST, preferred_element_type=F32
    )


def pack_kernel(
    h_ref, f_ref, cls_ref, idx_ref, val_ref, var_ref, k_ref, cnt_ref,
    up_ref, dn_ref, own_ref, edge_ref,
):
    cls = cls_ref[...]
    kc = jnp.zeros(cls.shape, F32)
    for index in range(12):
        kc = jnp.where(cls == index, k_ref[index], kc)
    own_ref[pl.ds(PAD, CELLS), :] = kc
    up_ref[pl.ds(MSG_KC, CELLS), :] = kc
    dn_ref[pl.ds(MSG_KC, CELLS), :] = kc
    kedge = edge_pack(
        lambda l, r: None
        if l == LEV
        else jnp.broadcast_to(kc[l * ROWS + r : l * ROWS + r + 1, :], (8, COLS))
    )
    edge_ref[pl.ds(MEM, 8), :] = kedge
    own_ref[pl.ds(MEM, 8), :] = kedge
    up_ref[pl.ds(MSG_EDGE + MEM, 8), :] = kedge
    dn_ref[pl.ds(MSG_EDGE + MEM, 8), :] = kedge

    own_ref[pl.ds(PAD + CELLS, 2 * CELLS), :] = scatter_obs(
        idx_ref, val_ref, var_ref, cnt_ref[0]
    )
    for g in range(GROUPS):
        h = {}
        for l in range(LEV):
            for r in range(ROWS):
                block = h_ref[pl.ds(g * 8 * CELLS + l * ROWS + r, 8, stride=CELLS), :]
                h[l, r] = block
                if r < HALO:
                    up_ref[pl.ds((l * HALO + r) * MEM + g * 8, 8), :] = block
                if r >= ROWS - HALO:
                    dn_ref[pl.ds((l * HALO + r - 1) * MEM + g * 8, 8), :] = block
        for r in range(ROWS):
            block = f_ref[pl.ds(g * 8 * ROWS + r, 8, stride=ROWS), :]
            h[LEV, r] = block
            if r < 2:
                up_ref[pl.ds(MSG_FORCE + r * MEM + g * 8, 8), :] = block
            else:
                dn_ref[pl.ds(MSG_FORCE + (r - 2) * MEM + g * 8, 8), :] = block
        edge = edge_pack(lambda l, r: h[l, r])
        edge_ref[pl.ds(g * 8, 8), :] = edge
        own_ref[pl.ds(g * 8, 8), :] = edge
        up_ref[pl.ds(MSG_EDGE + g * 8, 8), :] = edge
        dn_ref[pl.ds(MSG_EDGE + g * 8, 8), :] = edge


def forecast_kernel(
    regions, tiles,
    h_ref, f_ref, own_ref, above_ref, below_ref, el_ref, er_ref,
    uel_ref, uer_ref, del_ref, der_ref,
    dev_ref, mean_ref, pay_ref,
    z_ref, ks_ref, kr_ref, face_ref, hold_ref, gram_ref,
):
    ri = lax.axis_index("region")
    ti = lax.axis_index("tile")
    top_ok = jnp.where(ri > 0, 1.0, 0.0)
    bot_ok = jnp.where(ri < regions - 1, 1.0, 0.0)
    left_ok = jnp.where(ti > 0, 1.0, 0.0)
    right_ok = jnp.where(ti < tiles - 1, 1.0, 0.0)
    lane = lanes()
    half = lane % 64
    srow = half // 6
    scol = half % 6
    is_left = lane < 64
    row_ok = jnp.where(srow < HALO, top_ok, jnp.where(srow >= HALO + ROWS, bot_ok, 1.0))
    side_ok = jnp.where(
        is_left, jnp.where(scol < 3, left_ok, 1.0), jnp.where(scol >= 3, right_ok, 1.0)
    )
    smask = jnp.where(half < 60, row_ok * side_ok, 0.0)
    low_k = lane % 6 < 3

    def strips(base):
        own, left, right = base(own_ref, 0), base(el_ref, 0), base(er_ref, 0)
        uown, ul, ur = base(above_ref, MSG_EDGE), base(uel_ref, 0), base(uer_ref, 0)
        down, dl, dr = base(below_ref, MSG_EDGE), base(del_ref, 0), base(der_ref, 0)
        parts = (
            (jnp.where(low_k, ul, uown), jnp.where(low_k, uown, ur), -1),
            (jnp.where(low_k, left, own), jnp.where(low_k, own, right), 3),
            (jnp.where(low_k, dl, down), jnp.where(low_k, down, dr), 7),
        )
        out = []
        for l in range(LEV + 1):
            strip = jnp.zeros((8, COLS), F32)
            for lo, hi, first in parts:
                inside = (srow >= first) & (srow < first + ROWS)
                strip = jnp.where(inside & is_left, roll(lo, first * 6 - l * 24), strip)
                strip = jnp.where(inside & ~is_left, roll(hi, 64 + first * 6 - l * 24), strip)
            out.append(strip * smask)
        return out

    kstrip = strips(lambda ref, base: ref[pl.ds(base + MEM, 8), :])
    def kc_row(l, e):
        r = e - HALO
        if r < 0:
            at = MSG_KC + l * ROWS + r + ROWS
            return above_ref[at : at + 1, :] * top_ok
        if r >= ROWS:
            at = MSG_KC + l * ROWS + r - ROWS
            return below_ref[at : at + 1, :] * bot_ok
        at = PAD + l * ROWS + r
        return own_ref[at : at + 1, :]

    for l in range(LEV):
        ks_ref[pl.ds(l * 8, 8), :] = 0.0625 * kstrip[l]
        for e in range(EXT):
            kr_ref[pl.ds((l * EXT + e) * 8, 8), :] = jnp.broadcast_to(
                0.0625 * kc_row(l, e), (8, COLS)
            )

    def conduct(kc, h):
        return kc * (2.0 + jnp.tanh(0.5 * h))

    joint = is_left & (scol == 1)

    def group(g, carry):
        base = g * 8

        def prior_row(l, e):
            r = e - HALO
            if r < 0:
                at = (l * HALO + r + HALO) * MEM
                return above_ref[pl.ds(at + base, 8), :] * top_ok
            if r >= ROWS:
                at = (l * HALO + r - ROWS) * MEM
                return below_ref[pl.ds(at + base, 8), :] * bot_ok
            return h_ref[pl.ds(g * (8 * CELLS) + l * ROWS + r, 8, stride=CELLS), :]

        def force_row(e):
            r = e - HALO
            if r < 0:
                return above_ref[pl.ds(MSG_FORCE + (r + 2) * MEM + base, 8), :]
            if r >= ROWS:
                return below_ref[pl.ds(MSG_FORCE + (r - ROWS) * MEM + base, 8), :]
            return f_ref[pl.ds(g * (8 * ROWS) + r, 8, stride=ROWS), :]

        hs = strips(lambda ref, first: ref[pl.ds(first + base, 8), :])
        fs = hs[LEV]
        for step in range(STEPS):
            sk = [conduct(ks_ref[pl.ds(l * 8, 8), :], hs[l]) for l in range(LEV)]
            faces = [
                (sk[l] + roll(sk[l], -1)) * (roll(hs[l], -1) - hs[l]) for l in range(LEV)
            ]
            for l in range(LEV):
                edge = jnp.where(joint, roll(faces[l], -65), faces[l])
                face_ref[pl.ds((step * LEV + l) * 8, 8), :] = edge
            if step == STEPS - 1:
                break
            fresh = []
            last = None
            for l in range(LEV):
                down = (sk[l] + roll(sk[l], -6)) * (roll(hs[l], -6) - hs[l])
                flux = (faces[l] - roll(faces[l], 1)) + (down - roll(down, 6))
                if l > 0:
                    flux = flux - last
                if l < LEV - 1:
                    last = 0.5 * (sk[l] + sk[l + 1]) * (hs[l + 1] - hs[l])
                    flux = flux + last
                if l == 0:
                    flux = flux + 0.25 * fs
                fresh.append((hs[l] + flux) * smask)
            hs = fresh

        for step in range(STEPS):
            def row(l, e):
                if step == 0:
                    return prior_row(l, e)
                return hold_ref[step - 1, pl.ds((l * EXT + e) * 8, 8), :]

            h_now = k_now = face_now = None
            for e in range(step, EXT - step):
                h_new = [row(l, e) for l in range(LEV)]
                k_new = [
                    conduct(kr_ref[pl.ds((l * EXT + e) * 8, 8), :], h_new[l])
                    for l in range(LEV)
                ]
                face_new = None
                if e > step:
                    face_new = [
                        (k_now[l] + k_new[l]) * (h_new[l] - h_now[l]) for l in range(LEV)
                    ]
                if e > step + 1:
                    at = e - 1
                    r = at - HALO
                    last = None
                    for l in range(LEV):
                        here, kh = h_now[l], k_now[l]
                        edge = roll(
                            face_ref[pl.ds((step * LEV + l) * 8, 8), :], -(at * 6 + 2)
                        )
                        face = (kh + roll(kh, -1)) * (roll(here, -1) - here)
                        face = jnp.where(lane == COLS - 1, edge, face)
                        behind = jnp.where(lane == 0, edge, roll(face, 1))
                        flux = (face - behind) + (face_new[l] - face_now[l])
                        if l > 0:
                            flux = flux - last
                        if l < LEV - 1:
                            last = 0.5 * (kh + k_now[l + 1]) * (h_now[l + 1] - here)
                            flux = flux + last
                        if l == 0:
                            flux = flux + 0.25 * force_row(at)
                        value = here + flux
                        if step == STEPS - 1:
                            lr = l * ROWS + r
                            dev_ref[pl.ds(base, 8), lr * COLS : (lr + 1) * COLS] = value
                            continue
                        if r < 0:
                            value = value * top_ok
                        elif r >= ROWS:
                            value = value * bot_ok
                        hold_ref[step, pl.ds((l * EXT + at) * 8, 8), :] = value
                h_now, k_now, face_now = h_new, k_new, face_new
        return carry

    lax.fori_loop(0, GROUPS, group, 0)

    for lr in range(CELLS):
        cols = slice(lr * COLS, (lr + 1) * COLS)
        head = dev_ref[:, cols]
        mean = jnp.sum(head, axis=0, keepdims=True) * (1.0 / MEM)
        mean_ref[lr : lr + 1, :] = mean
        dev = head - mean
        dev_ref[:, cols] = dev
        scale = own_ref[PAD + CELLS + lr : PAD + CELLS + lr + 1, :]
        z_ref[0:MEM, cols] = dev * scale
        rest = own_ref[PAD + 2 * CELLS + lr : PAD + 2 * CELLS + lr + 1, :] - scale * mean
        z_ref[MEM : MEM + 8, cols] = jnp.broadcast_to(rest, (8, COLS))
    gram_ref[:, 0:MEM] = lax.dot_general(
        z_ref[...], dev_ref[...], (((1,), (1,)), ((), ())),
        precision=HIGHEST, preferred_element_type=F32,
    )
    gram_ref[:, MEM:COLS] = jnp.zeros((PAD, COLS - MEM), F32)

    vec = gram_ref[MEM:PAD, :]
    sub = lax.broadcasted_iota(jnp.int32, (8, COLS), 0)

    def stripe(i):
        block = gram_ref[8 * i : 8 * i + 8, :]
        block = jnp.where((sub == 7) & (lane >= 8 * i) & (lane < 8 * i + 7), vec, block)
        return jnp.where((sub == 6) & (lane == 8 * i + 5), roll(vec, -2), block)

    def joined(i):
        if i == 0:
            return stripe(0)
        return jnp.where(lane >= 8 * i, stripe(i), roll(stripe(8 - i), 8 * i - MEM))

    first = jnp.where(lane < MEM, joined(0), roll(joined(1), MEM))
    second = jnp.where(lane < MEM, joined(2), roll(joined(3), MEM))
    middle = stripe(4)
    third = roll(middle, -32)[0:2]
    for q in range(1, 4):
        third = jnp.where(
            lane[0:2] >= 32 * q, roll(middle, 32 * q - 32)[2 * q : 2 * q + 2], third
        )
    pieces = [block[2 * q : 2 * q + 2] for block in (first, second) for q in range(4)]
    for i, piece in enumerate(pieces + [third]):
        for c in range(tiles):
            pay_ref[c, :, i * COLS : (i + 1) * COLS] = piece


def analysis_kernel(copies, pay_ref, dev_ref, mean_ref, out_ref, m_ref):
    lane = lanes()
    sub = lax.broadcasted_iota(jnp.int32, (8, COLS), 0)
    total = pay_ref[0]
    for c in range(1, copies):
        total = total + pay_ref[c]
    piece = [total[:, i * COLS : (i + 1) * COLS] for i in range(9)]
    first = jnp.concatenate(piece[0:4], axis=0)
    second = jnp.concatenate(piece[4:8], axis=0)
    halves = [
        first,
        roll(first, MEM),
        second,
        roll(second, MEM),
        jnp.concatenate([roll(piece[8], 32 - 32 * q) for q in range(4)], axis=0),
    ]
    bvec = jnp.zeros((1, COLS), F32)
    for i in range(8):
        block = halves[i] if i <= 4 else roll(halves[8 - i], MEM - 8 * (8 - i))
        here = lane[0:1] // 8 == i
        tail = jnp.where(lane[0:1] % 8 == 7, roll(block, 2)[6:7], block[7:8])
        bvec = jnp.where(here, tail, bvec)
        keep = (lane >= sub + 8 * i) & (lane < MEM)
        block = jnp.where(keep, block, 0.0)
        block = block + jnp.where(lane == sub + 8 * i, MEM - 1.0, 0.0)
        block = block + jnp.where(lane == sub + (8 * i + MEM), 1.0, 0.0)
        m_ref[8 * i : 8 * i + 8, :] = block
    bvec = roll(bvec, MEM)

    for kb in range(8):
        block = m_ref[8 * kb : 8 * kb + 8, :]
        at = 8 * kb
        full = {
            (i, j): jnp.broadcast_to(block[j : j + 1, at + i : at + i + 1], (8, COLS))
            for i in range(8)
            for j in range(i + 1)
        }
        for j in range(8):
            inv = lax.rsqrt(full[j, j])
            low = {i: full[i, j] * inv for i in range(j + 1, 8)}
            for i in range(j + 1, 8):
                for m in range(j + 1, i + 1):
                    full[i, m] = full[i, m] - low[i] * low[m]
            prow = jnp.broadcast_to(block[j : j + 1, :], (8, COLS)) * inv
            column = jnp.zeros((8, COLS), F32)
            for i in range(j + 1, 8):
                column = jnp.where(sub == i, low[i], column)
            block = jnp.where(sub == j, prow, block - column * prow)
        m_ref[8 * kb : 8 * kb + 8, :] = block
        if kb < 7:
            later = 8 * (kb + 1)
            update = lax.dot_general(
                block[:, 0:MEM], block, (((0,), (0,)), ((), ())),
                precision=HIGHEST, preferred_element_type=F32,
            )
            m_ref[later:MEM, :] = m_ref[later:MEM, :] - update[later:MEM, :]

    inverse = m_ref[...]
    bvec = jnp.where(lane[0:1] >= MEM, bvec, 0.0)
    y = jnp.sum(inverse * bvec, axis=1, keepdims=True)
    w = jnp.sum(inverse * y, axis=0, keepdims=True)
    blend = (inverse * jnp.sqrt(jnp.full((1, COLS), MEM - 1.0, F32)) + w)[:, MEM:COLS]
    for lr in range(0, CELLS, 2):
        both = jnp.dot(
            blend, dev_ref[:, lr * COLS : (lr + 2) * COLS],
            precision=HIGHEST, preferred_element_type=F32,
        )
        for i in range(2):
            value = mean_ref[lr + i : lr + i + 1, :] + both[:, i * COLS : (i + 1) * COLS]
            out_ref[pl.ds(lr + i, MEM, stride=CELLS), :] = value


def vmem():
    return pl.BlockSpec(memory_space=pltpu.VMEM)


def smem():
    return pl.BlockSpec(memory_space=pltpu.SMEM)


PARAMS = pltpu.CompilerParams(vmem_limit_bytes=32 * 1024 * 1024)


def shift(x, axis, by, wrap=True):
    count = lax.axis_size(axis)
    pairs = [(i, (i + by) % count) for i in range(count) if wrap or 0 <= i + by < count]
    return lax.ppermute(x, axis, pairs)


def shards(prior, source, soil_class, soil_k, obs_index, obs_value, obs_var, obs_count):
    regions, tiles = lax.axis_size("region"), lax.axis_size("tile")
    prior = prior.reshape(MEM * CELLS, COLS)
    source = source.reshape(MEM * ROWS, COLS)
    soil_class = soil_class.reshape(CELLS, COLS)
    slots = obs_index.shape[0]

    def out(*shape):
        return jax.ShapeDtypeStruct(shape, F32)

    up, dn, own, edge = pl.pallas_call(
        pack_kernel,
        out_shape=(
            out(MSG_ROWS, COLS), out(MSG_ROWS, COLS), out(PAD + 3 * CELLS, COLS), out(PAD, COLS)
        ),
        in_specs=[vmem()] * 6 + [smem()] * 2,
        out_specs=(vmem(),) * 4,
        compiler_params=PARAMS,
        name="pack",
    )(
        prior, source, soil_class,
        obs_index.reshape(1, slots), obs_value.reshape(1, slots), obs_var.reshape(1, slots),
        soil_k, obs_count,
    )
    above = shift(dn, "region", 1)
    below = shift(up, "region", -1)
    el = shift(edge, "tile", 1, False)
    er = shift(edge, "tile", -1, False)
    uel, uer = shift(el, "region", 1), shift(er, "region", 1)
    bel, ber = shift(el, "region", -1), shift(er, "region", -1)
    dev, mean, pay = pl.pallas_call(
        functools.partial(forecast_kernel, regions, tiles),
        out_shape=(out(MEM, CELLS * COLS), out(CELLS, COLS), out(tiles, 2, PAYLOAD)),
        in_specs=[vmem()] * 11,
        out_specs=(vmem(),) * 3,
        scratch_shapes=[
            pltpu.VMEM((PAD, CELLS * COLS), F32),
            pltpu.VMEM((LEV * 8, COLS), F32),
            pltpu.VMEM((LEV * EXT * 8, COLS), F32),
            pltpu.VMEM((STEPS * LEV * 8, COLS), F32),
            pltpu.VMEM((STEPS - 1, LEV * EXT * 8, COLS), F32),
            pltpu.VMEM((PAD, COLS), F32),
        ],
        compiler_params=PARAMS,
        name="forecast",
    )(prior, source, own, above, below, el, er, uel, uer, bel, ber)
    part = lax.all_to_all(pay, "tile", 0, 0).sum(axis=0)
    pay = lax.all_to_all(jnp.broadcast_to(part, (regions,) + part.shape), "region", 0, 0)
    result = pl.pallas_call(
        functools.partial(analysis_kernel, regions),
        out_shape=out(MEM * CELLS, COLS),
        in_specs=[vmem()] * 3,
        out_specs=vmem(),
        scratch_shapes=[pltpu.VMEM((MEM, COLS), F32)],
        compiler_params=PARAMS,
        name="analysis",
    )(pay, dev, mean)
    return result.reshape(MEM, LEV, ROWS, COLS)


def solution(mesh):
    return jax.shard_map(
        shards,
        mesh=mesh,
        in_specs=(
            P(None, None, "region", "tile"),
            P(None, "region", "tile"),
            P(None, "region", "tile"),
            P(),
            P(("region", "tile")),
            P(("region", "tile")),
            P(("region", "tile")),
            P(("region", "tile")),
        ),
        out_specs=P(None, None, "region", "tile"),
        check_vma=False,
    )
```
